32 devices in a mesh: seq: 4 (over y, x), kvh: 2 (over core), rep: 4 (over z).
Axes of the slice: x: 2, y: 2, z: 4, core: 2. Of those that a mesh axis runs over, the one named last changes fastest.
Arguments:
- queries: bfloat16 [32, 2, 4, 128], P('rep', 'kvh'), parts along dimension 0, may hold values from -6 to 6
- slot_key_cache: bfloat16 [32, 2, 1024, 128], P('rep', 'kvh', 'seq'), parts along dimension 0, may hold values from -6 to 6
- slot_value_cache: bfloat16 [32, 2, 1024, 128], P('rep', 'kvh', 'seq'), parts along dimension 0, may hold values from -24 to 24
- lengths: int32 [32], P('rep'), parts along dimension 0, may hold values from 128 to 1024, as said below
- output_weight_matrix: bfloat16 [2, 4, 128, 8192], P('kvh', 'seq'), may hold values from -0.25 to 0.25
- residual: float32 [32, 8192], P('rep', ('seq', 'kvh')), parts along dimension 0, may hold values from -6 to 6
Outputs:
- hidden_out: float32 [32, 8192], P('rep', ('seq', 'kvh')), parts along dimension 0
The draws below stay inside these ranges and needn't reach their ends.
There are 4 independent parts, one for each index of `rep`. The reference program is written for one: setup_inputs(seed, part) draws one part's arguments, and reference() takes and returns one part's arrays. A program takes and returns all parts, laid end to end along the dimension named above; an argument that names none is the same for every part. Nothing has to cross between parts.
Inputs may be any that keep to these rules, and one draw needn't show every extreme that they name: Some row has 1024 live positions and some row 128; a row's live block count is lengths rounded up to whole blocks of 32.
All inputs are finite; a program needn't handle non-finite values.
Results may differ from the reference program's by a relative error of at most 0.0028.
Values sent between devices are 32-bit elements; how exact they have to be, the bound alone decides.
A program may use at most 64 MiB of HBM per device.

```python
import math
import jax
import jax.numpy as jnp
from jax import lax

HEAD_DIMENSION = 128
OUTPUT_FEATURES = 8192
DECODE_ROWS = 8
SHARD_SLOTS = 256
BLOCK_POSITIONS = 32
CACHE_SHARDS = 4
QUERY_PER_KEY = 4
KEY_HEADS = 2
CONTEXT_SLOTS = 1024
SHORTEST = 128


def draw_slot_key_cache(key, part):
    random_root_key = jax.random.fold_in(key, 11)
    value_vectors = jax.random.normal(random_root_key, (DECODE_ROWS, KEY_HEADS, CONTEXT_SLOTS, HEAD_DIMENSION), jnp.float32)
    return jnp.clip(value_vectors, -6.0, 6.0).astype(jnp.bfloat16)


def draw_queries(key, part):
    random_root_key = jax.random.fold_in(key, 13)
    value_vectors = jax.random.normal(random_root_key, (DECODE_ROWS, KEY_HEADS, QUERY_PER_KEY, HEAD_DIMENSION), jnp.float32)
    return jnp.clip(value_vectors, -6.0, 6.0).astype(jnp.bfloat16)


def draw_lengths(key, part):
    drawn = jax.random.randint(jax.random.fold_in(key, 3), (DECODE_ROWS,), SHORTEST, CONTEXT_SLOTS + 1)
    ordering = jax.random.permutation(jax.random.fold_in(key, 5), DECODE_ROWS)
    drawn = drawn.at[ordering[0]].set(CONTEXT_SLOTS)
    drawn = drawn.at[ordering[1]].set(SHORTEST)
    return drawn.astype(jnp.int32)


def block_scale(stream_key, extent, cuts, low, largest):
    gain = 1.0
    for dim, parts in cuts:
        steps = jax.random.uniform(jax.random.fold_in(jax.random.fold_in(stream_key, 6), dim), (parts,), jnp.float32, low / len(cuts), largest / len(cuts))
        gain = gain * jnp.repeat(jnp.exp(steps), extent[dim] // parts).reshape((-1,) + (1,) * (len(extent) - 1 - dim))
    return gain


def bell_draw(stream_key, dims, deviation, reach, pieces=(), held_as=jnp.bfloat16):
    level = block_scale(stream_key, dims, pieces, -0.22, 0.18) if pieces else 1.0
    array = jax.random.normal(stream_key, dims, jnp.float32) * deviation * level
    return jnp.minimum(jnp.maximum(array, -reach), reach).astype(held_as)


def setup_inputs(seed: int = 0, part: int = 0) -> dict:
    key_of = jax.random.split(jax.random.key(seed), 7)
    own_keys = jax.random.split(jax.random.fold_in(key_of[6], part), 7)
    queries = draw_queries(jax.random.fold_in(jax.random.fold_in(key_of[6], part), 71), part)
    slot_key_cache = draw_slot_key_cache(jax.random.fold_in(jax.random.fold_in(key_of[6], part), 71), part)
    slot_value_cache = bell_draw(own_keys[2], (DECODE_ROWS, KEY_HEADS, CONTEXT_SLOTS, HEAD_DIMENSION), 4.0, 24.0, ((1, 2), (2, 4)))
    lengths = draw_lengths(jax.random.fold_in(jax.random.fold_in(key_of[6], part), 71), part)
    output_weight_matrix = bell_draw(key_of[4], (KEY_HEADS, QUERY_PER_KEY, HEAD_DIMENSION, OUTPUT_FEATURES), (QUERY_PER_KEY * HEAD_DIMENSION) ** -0.5, 0.25, ((0, 2), (1, 4)))
    residual = bell_draw(own_keys[5], (DECODE_ROWS, OUTPUT_FEATURES), 1.0, 6.0, ((1, 8),), jnp.float32)
    return dict(queries=queries, slot_key_cache=slot_key_cache, slot_value_cache=slot_value_cache, lengths=lengths, output_weight_matrix=output_weight_matrix, residual=residual)


def reference(queries, slot_key_cache, slot_value_cache, lengths, output_weight_matrix, residual):
    scale = 1.0 / math.sqrt(HEAD_DIMENSION)
    gathered_keys = slot_key_cache.astype(jnp.float32).reshape(DECODE_ROWS, KEY_HEADS, CACHE_SHARDS, SHARD_SLOTS, HEAD_DIMENSION)
    gathered_values = slot_value_cache.astype(jnp.float32).reshape(DECODE_ROWS, KEY_HEADS, CACHE_SHARDS, SHARD_SLOTS, HEAD_DIMENSION)
    slot_local = jnp.arange(SHARD_SLOTS, dtype=jnp.int32)
    shard_ids = jnp.arange(CACHE_SHARDS, dtype=jnp.int32)
    positions = (slot_local[None, :] // BLOCK_POSITIONS * CACHE_SHARDS + shard_ids[:, None]) * BLOCK_POSITIONS + slot_local[None, :] % BLOCK_POSITIONS
    visible = positions[None, :, :] < lengths.astype(jnp.int32)[:, None, None]
    scores = jnp.einsum('bkgd,bkscd->bkgsc', queries.astype(jnp.float32), gathered_keys) * scale
    scores = jnp.where(visible[:, None, None, :, :], scores, -1e+30)
    maximum = lax.optimization_barrier(jnp.max(scores, axis=-1))
    weights = jnp.exp(scores - maximum[..., None])
    totals = lax.optimization_barrier(jnp.sum(weights, axis=-1))
    rounded = lax.optimization_barrier(weights.astype(jnp.bfloat16)).astype(jnp.float32)
    summed = jnp.einsum('bkgsc,bkscd->bkgsd', rounded, gathered_values)
    partial_value = summed / totals[..., None]
    log_sums = maximum + jnp.log(totals)
    highest = lax.optimization_barrier(jnp.max(log_sums, axis=3))
    factors = jnp.exp(log_sums - highest[..., None])
    attention_output = lax.optimization_barrier(jnp.sum(factors[..., None] * partial_value, axis=3)) / lax.optimization_barrier(jnp.sum(factors, axis=3))[..., None]
    flattened_attention = attention_output.astype(jnp.bfloat16).reshape(DECODE_ROWS, KEY_HEADS * QUERY_PER_KEY * HEAD_DIMENSION)
    projected_output = jnp.dot(flattened_attention, output_weight_matrix.reshape(KEY_HEADS * QUERY_PER_KEY * HEAD_DIMENSION, OUTPUT_FEATURES), preferred_element_type=jnp.float32)
    return residual + projected_output
```

```python
import functools
import math

import jax
import jax.numpy as jnp
from jax import lax
from jax.experimental import pallas as pl
from jax.experimental.pallas import tpu as pltpu
from jax.sharding import PartitionSpec as P

BLOCK_POSITIONS = 32
MESH = pl.DeviceIdType.MESH


def partner(me, step, count):
    result = 0
    bit = 1
    while bit < count:
        own = lax.rem(lax.div(me, bit), 2)
        result = result + bit * (1 - own if (step // bit) % 2 else own)
        bit *= 2
    return result


def kernel(
    n_seq, n_kvh,
    lengths, queries, keys, values, weights, residual, out,
    q_buf, q_rows, k_buf, v_buf, w_buf, r_buf,
    part_send, part_recv, core_send, core_recv, seq_send, seq_recv, contrib,
    load_sem, ps_sem, pr_sem, cs_sem, cr_sem, ss_sem, sr_sem,
):
    seq = lax.axis_index("seq")
    kvh = lax.axis_index("kvh")
    rows, _, heads, size = queries.shape
    slots = keys.shape[2]
    share = out.shape[1]
    blocks = n_seq * n_kvh

    loads = [
        pltpu.make_async_copy(queries, q_buf, load_sem.at[0]),
        pltpu.make_async_copy(keys, k_buf, load_sem.at[1]),
        pltpu.make_async_copy(values, v_buf, load_sem.at[2]),
        pltpu.make_async_copy(weights.at[0, 0], w_buf, load_sem.at[3]),
        pltpu.make_async_copy(residual, r_buf, load_sem.at[4]),
    ]
    for load in loads:
        load.start()

    seq_peers = [partner(seq, i, n_seq) for i in range(n_seq)]
    kvh_peers = [partner(kvh, j, n_kvh) for j in range(n_kvh)]
    barrier = pltpu.get_barrier_semaphore()
    for i in range(1, n_seq):
        pl.semaphore_signal(barrier, inc=1, device_id={"seq": seq_peers[i]}, device_id_type=MESH)
    for j in range(1, n_kvh):
        pl.semaphore_signal(barrier, inc=1, device_id={"kvh": kvh_peers[j]}, device_id_type=MESH)

    row = lax.broadcasted_iota(jnp.int32, (rows, slots), 0)
    slot = lax.broadcasted_iota(jnp.int32, (rows, slots), 1)
    length = jnp.zeros((rows, slots), jnp.int32)
    for b in range(rows):
        length = jnp.where(row == b, lengths[b], length)
    position = (slot // BLOCK_POSITIONS * n_seq + seq) * BLOCK_POSITIONS + slot % BLOCK_POSITIONS
    live = position < length
    out_row = lax.broadcasted_iota(jnp.int32, (rows, size), 0)

    loads[0].wait()
    for b in range(rows):
        q_rows[pl.ds(b * heads, heads), :] = q_buf[b, 0].astype(jnp.float32)
    q = jnp.concatenate(
        [q_rows[pl.ds(g, rows, stride=heads), :] for g in range(heads)], axis=0
    ).astype(jnp.bfloat16)

    loads[1].wait()
    scores = jnp.zeros((heads, rows, slots), jnp.float32)
    for b in range(rows):
        full = lax.dot_general(
            q, k_buf[b, 0], (((1,), (1,)), ((), ())), preferred_element_type=jnp.float32
        ).reshape(heads, rows, slots)
        scores = jnp.where((row == b)[None], full, scores)
    scores = jnp.where(live[None], scores * (1.0 / math.sqrt(size)), -1e30)
    top = jnp.max(scores, axis=2, keepdims=True)
    probs = jnp.exp(scores - top)
    total = jnp.sum(probs, axis=2, keepdims=True)
    probs = probs.reshape(heads * rows, slots).astype(jnp.bfloat16)
    loads[2].wait()
    summed = jnp.zeros((heads, rows, size), jnp.float32)
    for b in range(rows):
        full = jnp.dot(probs, v_buf[b, 0], preferred_element_type=jnp.float32)
        summed = jnp.where((out_row == b)[None], full.reshape(heads, rows, size), summed)
    part_send[:, :rows, :] = summed / total
    part_send[:, rows:, :] = jnp.broadcast_to(top + jnp.log(total), (heads, rows, size))

    pl.semaphore_wait(barrier, n_seq - 1 + n_kvh - 1)
    sends = []
    order = list(range(n_seq - 1, 0, -1))
    part_copies = {}
    for i in order:
        copy = pltpu.make_async_remote_copy(
            src_ref=part_send.at[seq_peers[i]],
            dst_ref=part_recv.at[i],
            send_sem=ps_sem.at[i],
            recv_sem=pr_sem.at[i],
            device_id={"seq": seq_peers[i]},
            device_id_type=MESH,
        )
        copy.start()
        part_copies[i] = copy
        sends.append(copy)

    loads[3].wait()
    loads[4].wait()
    parts = [part_send[seq]]
    for i in range(1, n_seq):
        part_copies[i].wait_recv()
        parts.append(part_recv[i])
    highest = functools.reduce(jnp.maximum, [part[rows:] for part in parts])
    factors = [jnp.exp(part[rows:] - highest) for part in parts]
    joined = sum(factor * part[:rows] for factor, part in zip(factors, parts))
    attended = (joined / sum(factors)).astype(jnp.bfloat16)

    aligned = share % 128 == 0
    if not aligned:
        for first in range(0, blocks * share, 1024):
            tile = jnp.dot(
                attended, w_buf[:, first:first + 1024], preferred_element_type=jnp.float32
            )
            for block in range(1024 // share):
                contrib[first // share + block] = tile[:, block * share:(block + 1) * share]

    def contribution(i, j):
        block = seq_peers[i] * n_kvh + kvh_peers[j]
        if not aligned:
            return contrib[block]
        columns = pl.ds(pl.multiple_of(block * share, share), share)
        return jnp.dot(attended, w_buf[:, columns], preferred_element_type=jnp.float32)

    order.append(0)
    core_copies = {}
    for i in order:
        for j in range(1, n_kvh):
            core_send[i, j] = contribution(i, j)
            copy = pltpu.make_async_remote_copy(
                src_ref=core_send.at[i, j],
                dst_ref=core_recv.at[i, j],
                send_sem=cs_sem.at[i, j],
                recv_sem=cr_sem.at[i, j],
                device_id={"kvh": kvh_peers[j]},
                device_id_type=MESH,
            )
            copy.start()
            core_copies[i, j] = copy
            sends.append(copy)
    seq_copies = {}
    for i in order:
        own = contribution(i, 0)
        for j in range(1, n_kvh):
            core_copies[i, j].wait_recv()
            own = own + core_recv[i, j]
        if i:
            seq_send[i] = own
            copy = pltpu.make_async_remote_copy(
                src_ref=seq_send.at[i],
                dst_ref=seq_recv.at[i],
                send_sem=ss_sem.at[i],
                recv_sem=sr_sem.at[i],
                device_id={"seq": seq_peers[i]},
                device_id_type=MESH,
            )
            copy.start()
            seq_copies[i] = copy
            sends.append(copy)
        else:
            result = r_buf[...] + own
    for i in order[:-1][::-1]:
        seq_copies[i].wait_recv()
        result = result + seq_recv[i]
    out[...] = result
    for copy in sends:
        copy.wait_send()


def body(n_seq, n_kvh, queries, keys, values, lengths, weights, residual):
    rows, _, heads, size = queries.shape
    slots = keys.shape[2]
    features = weights.shape[3]
    share = residual.shape[1]
    f32, bf16 = jnp.float32, jnp.bfloat16
    dma = pltpu.SemaphoreType.DMA
    in_hbm = pl.BlockSpec(memory_space=pltpu.HBM)
    return pl.pallas_call(
        functools.partial(kernel, n_seq, n_kvh),
        out_shape=jax.ShapeDtypeStruct((rows, share), f32),
        in_specs=[pl.BlockSpec(memory_space=pltpu.SMEM)] + [in_hbm] * 5,
        out_specs=pl.BlockSpec(memory_space=pltpu.VMEM),
        scratch_shapes=[
            pltpu.VMEM((rows, 1, heads, size), bf16),
            pltpu.VMEM((rows * heads, size), f32),
            pltpu.VMEM((rows, 1, slots, size), bf16),
            pltpu.VMEM((rows, 1, slots, size), bf16),
            pltpu.VMEM((size, features), bf16),
            pltpu.VMEM((rows, share), f32),
            pltpu.VMEM((heads, 2 * rows, size), f32),
            pltpu.VMEM((n_seq, 2 * rows, size), f32),
            pltpu.VMEM((n_seq, n_kvh, rows, share), f32),
            pltpu.VMEM((n_seq, n_kvh, rows, share), f32),
            pltpu.VMEM((n_seq, rows, share), f32),
            pltpu.VMEM((n_seq, rows, share), f32),
            pltpu.VMEM((n_seq * n_kvh if share % 128 else 1, rows, share), f32),
            dma((5,)),
            dma((n_seq,)),
            dma((n_seq,)),
            dma((n_seq, n_kvh)),
            dma((n_seq, n_kvh)),
            dma((n_seq,)),
            dma((n_seq,)),
        ],
        compiler_params=pltpu.CompilerParams(
            collective_id=0, has_side_effects=True, vmem_limit_bytes=40 * 1024 * 1024
        ),
        cost_estimate=pl.CostEstimate(
            flops=2 * rows * size * features, bytes_accessed=2 * size * features, transcendentals=0
        ),
    )(lengths, queries, keys, values, weights, residual)


def solution(mesh):
    in_specs = (
        P("rep", "kvh", None, None),
        P("rep", "kvh", "seq", None),
        P("rep", "kvh", "seq", None),
        P("rep"),
        P("kvh", "seq", None, None),
        P("rep", ("seq", "kvh")),
    )
    out_specs = P("rep", ("seq", "kvh"))
    run = functools.partial(body, mesh.shape["seq"], mesh.shape["kvh"])
    return jax.shard_map(run, mesh=mesh, in_specs=in_specs, out_specs=out_specs, check_vma=False)
```

```python
import functools
import math

import jax
import jax.numpy as jnp
from jax import lax
from jax.experimental import pallas as pl
from jax.experimental.pallas import tpu as pltpu
from jax.sharding import PartitionSpec as P

BLOCK_POSITIONS = 32
MESH = pl.DeviceIdType.MESH


def partner(me, step, count):
    result = 0
    bit = 1
    while bit < count:
        own = lax.rem(lax.div(me, bit), 2)
        result = result + bit * (1 - own if (step // bit) % 2 else own)
        bit *= 2
    return result


def kernel(
    n_seq, n_kvh,
    lengths, queries, keys, values, weights, residual, out,
    l_buf, q_buf, q_rows, k_buf, v_buf, w_buf, r_buf,
    part_send, part_recv, core_send, core_recv, seq_send, seq_recv, contrib,
    load_sem, ps_sem, pr_sem, cs_sem, cr_sem, ss_sem, sr_sem,
):
    seq = lax.axis_index("seq")
    kvh = lax.axis_index("kvh")
    rows, _, heads, size = queries.shape
    slots = keys.shape[2]
    share = out.shape[1]
    blocks = n_seq * n_kvh

    loads = [
        pltpu.make_async_copy(queries, q_buf, load_sem.at[0]),
        pltpu.make_async_copy(keys, k_buf, load_sem.at[1]),
        pltpu.make_async_copy(values, v_buf, load_sem.at[2]),
        pltpu.make_async_copy(weights.at[0, 0], w_buf, load_sem.at[3]),
        pltpu.make_async_copy(residual, r_buf, load_sem.at[4]),
        pltpu.make_async_copy(lengths, l_buf, load_sem.at[5]),
    ]
    for n in (5, 0, 1, 2, 3, 4):
        loads[n].start()

    seq_peers = [partner(seq, i, n_seq) for i in range(n_seq)]
    kvh_peers = [partner(kvh, j, n_kvh) for j in range(n_kvh)]
    barrier = pltpu.get_barrier_semaphore()
    for i in range(1, n_seq):
        pl.semaphore_signal(barrier, inc=1, device_id={"seq": seq_peers[i]}, device_id_type=MESH)
    for j in range(1, n_kvh):
        pl.semaphore_signal(barrier, inc=1, device_id={"kvh": kvh_peers[j]}, device_id_type=MESH)

    row = lax.broadcasted_iota(jnp.int32, (rows, slots), 0)
    slot = lax.broadcasted_iota(jnp.int32, (rows, slots), 1)
    length = jnp.zeros((rows, slots), jnp.int32)
    loads[5].wait()
    for b in range(rows):
        length = jnp.where(row == b, l_buf[b], length)
    position = (slot // BLOCK_POSITIONS * n_seq + seq) * BLOCK_POSITIONS + slot % BLOCK_POSITIONS
    live = position < length
    out_row = lax.broadcasted_iota(jnp.int32, (rows, size), 0)

    loads[0].wait()
    for b in range(rows):
        q_rows[pl.ds(b * heads, heads), :] = q_buf[b, 0].astype(jnp.float32)
    q = jnp.concatenate(
        [q_rows[pl.ds(g, rows, stride=heads), :] for g in range(heads)], axis=0
    ).astype(jnp.bfloat16)

    loads[1].wait()
    scores = jnp.zeros((heads, rows, slots), jnp.float32)
    for b in range(rows):
        full = lax.dot_general(
            q, k_buf[b, 0], (((1,), (1,)), ((), ())), preferred_element_type=jnp.float32
        ).reshape(heads, rows, slots)
        scores = jnp.where((row == b)[None], full, scores)
    scores = jnp.where(live[None], scores * (1.0 / math.sqrt(size)), -1e30)
    top = jnp.max(scores, axis=2, keepdims=True)
    probs = jnp.exp(scores - top)
    total = jnp.sum(probs, axis=2, keepdims=True)
    probs = probs.reshape(heads * rows, slots).astype(jnp.bfloat16)
    loads[2].wait()
    summed = jnp.zeros((heads, rows, size), jnp.float32)
    for b in range(rows):
        full = jnp.dot(probs, v_buf[b, 0], preferred_element_type=jnp.float32)
        summed = jnp.where((out_row == b)[None], full.reshape(heads, rows, size), summed)
    part_send[:, :rows, :] = summed / total
    part_send[:, rows:, :] = jnp.broadcast_to(top + jnp.log(total), (heads, rows, size))

    pl.semaphore_wait(barrier, n_seq - 1 + n_kvh - 1)
    sends = []
    order = list(range(n_seq - 1, 0, -1))
    part_copies = {}
    for i in order:
        copy = pltpu.make_async_remote_copy(
            src_ref=part_send.at[seq_peers[i]],
            dst_ref=part_recv.at[i],
            send_sem=ps_sem.at[i],
            recv_sem=pr_sem.at[i],
            device_id={"seq": seq_peers[i]},
            device_id_type=MESH,
        )
        copy.start()
        part_copies[i] = copy
        sends.append(copy)

    loads[3].wait()
    loads[4].wait()
    parts = [part_send[seq]]
    for i in range(1, n_seq):
        part_copies[i].wait_recv()
        parts.append(part_recv[i])
    highest = functools.reduce(jnp.maximum, [part[rows:] for part in parts])
    factors = [jnp.exp(part[rows:] - highest) for part in parts]
    joined = sum(factor * part[:rows] for factor, part in zip(factors, parts))
    attended = (joined / sum(factors)).astype(jnp.bfloat16)

    aligned = share % 128 == 0
    if not aligned:
        for first in range(0, blocks * share, 1024):
            tile = jnp.dot(
                attended, w_buf[:, first:first + 1024], preferred_element_type=jnp.float32
            )
            for block in range(1024 // share):
                contrib[first // share + block] = tile[:, block * share:(block + 1) * share]

    def contribution(i, j):
        block = seq_peers[i] * n_kvh + kvh_peers[j]
        if not aligned:
            return contrib[block]
        columns = pl.ds(pl.multiple_of(block * share, share), share)
        return jnp.dot(attended, w_buf[:, columns], preferred_element_type=jnp.float32)

    order.append(0)
    core_copies = {}
    for i in order:
        for j in range(1, n_kvh):
            core_send[i, j] = contribution(i, j)
            copy = pltpu.make_async_remote_copy(
                src_ref=core_send.at[i, j],
                dst_ref=core_recv.at[i, j],
                send_sem=cs_sem.at[i, j],
                recv_sem=cr_sem.at[i, j],
                device_id={"kvh": kvh_peers[j]},
                device_id_type=MESH,
            )
            copy.start()
            core_copies[i, j] = copy
            sends.append(copy)
    seq_copies = {}
    seq_send[order[0]] = contribution(order[0], 0)
    for i, after in zip(order, order[1:] + [None]):
        if after is not None:
            seq_send[after] = contribution(after, 0)
        own = seq_send[i]
        for j in range(1, n_kvh):
            core_copies[i, j].wait_recv()
            own = own + core_recv[i, j]
        if i:
            seq_send[i] = own
            copy = pltpu.make_async_remote_copy(
                src_ref=seq_send.at[i],
                dst_ref=seq_recv.at[i],
                send_sem=ss_sem.at[i],
                recv_sem=sr_sem.at[i],
                device_id={"seq": seq_peers[i]},
                device_id_type=MESH,
            )
            copy.start()
            seq_copies[i] = copy
            sends.append(copy)
        else:
            result = r_buf[...] + own
    for i in order[:-1][::-1]:
        seq_copies[i].wait_recv()
        result = result + seq_recv[i]
    out[...] = result
    for copy in sends:
        copy.wait_send()


def body(n_seq, n_kvh, queries, keys, values, lengths, weights, residual):
    rows, _, heads, size = queries.shape
    slots = keys.shape[2]
    features = weights.shape[3]
    share = residual.shape[1]
    f32, bf16 = jnp.float32, jnp.bfloat16
    dma = pltpu.SemaphoreType.DMA
    in_hbm = pl.BlockSpec(memory_space=pltpu.HBM)
    return pl.pallas_call(
        functools.partial(kernel, n_seq, n_kvh),
        out_shape=jax.ShapeDtypeStruct((rows, share), f32),
        in_specs=[in_hbm] * 6,
        out_specs=pl.BlockSpec(memory_space=pltpu.VMEM),
        scratch_shapes=[
            pltpu.SMEM((rows,), jnp.int32),
            pltpu.VMEM((rows, 1, heads, size), bf16),
            pltpu.VMEM((rows * heads, size), f32),
            pltpu.VMEM((rows, 1, slots, size), bf16),
            pltpu.VMEM((rows, 1, slots, size), bf16),
            pltpu.VMEM((size, features), bf16),
            pltpu.VMEM((rows, share), f32),
            pltpu.VMEM((heads, 2 * rows, size), f32),
            pltpu.VMEM((n_seq, 2 * rows, size), f32),
            pltpu.VMEM((n_seq, n_kvh, rows, share), f32),
            pltpu.VMEM((n_seq, n_kvh, rows, share), f32),
            pltpu.VMEM((n_seq, rows, share), f32),
            pltpu.VMEM((n_seq, rows, share), f32),
            pltpu.VMEM((n_seq * n_kvh if share % 128 else 1, rows, share), f32),
            dma((6,)),
            dma((n_seq,)),
            dma((n_seq,)),
            dma((n_seq, n_kvh)),
            dma((n_seq, n_kvh)),
            dma((n_seq,)),
            dma((n_seq,)),
        ],
        compiler_params=pltpu.CompilerParams(
            collective_id=0, has_side_effects=True, vmem_limit_bytes=40 * 1024 * 1024
        ),
        cost_estimate=pl.CostEstimate(
            flops=2 * rows * size * features, bytes_accessed=2 * size * features, transcendentals=0
        ),
    )(*[
        pltpu.with_memory_space_constraint(array, pltpu.HBM)
        for array in (lengths, queries, keys, values, weights, residual)
    ])


def solution(mesh):
    in_specs = (
        P("rep", "kvh", None, None),
        P("rep", "kvh", "seq", None),
        P("rep", "kvh", "seq", None),
        P("rep"),
        P("kvh", "seq", None, None),
        P("rep", ("seq", "kvh")),
    )
    out_specs = P("rep", ("seq", "kvh"))
    run = functools.partial(body, mesh.shape["seq"], mesh.shape["kvh"])
    return jax.shard_map(run, mesh=mesh, in_specs=in_specs, out_specs=out_specs, check_vma=False)
```

```python
import functools
import math

import jax
import jax.numpy as jnp
from jax import lax
from jax.experimental import pallas as pl
from jax.experimental.pallas import tpu as pltpu
from jax.sharding import PartitionSpec as P

BLOCK_POSITIONS = 32
DIRECT_COLUMNS = 256
MESH = pl.DeviceIdType.MESH


def partner(me, step, count):
    result = 0
    bit = 1
    while bit < count:
        own = lax.rem(lax.div(me, bit), 2)
        result = result + bit * (1 - own if (step // bit) % 2 else own)
        bit *= 2
    return result


def kernel(
    n_seq, n_kvh, cut,
    lengths, queries, keys, values, weights, residual, out,
    l_buf, q_buf, q_rows, k_buf, v_buf, w_buf, r_buf,
    part_send, part_recv, direct_send, direct_recv, core_send, core_recv,
    seq_send, seq_recv, contrib,
    load_sem, ps_sem, pr_sem, ds_sem, dr_sem, cs_sem, cr_sem, ss_sem, sr_sem,
):
    seq = lax.axis_index("seq")
    kvh = lax.axis_index("kvh")
    rows, _, heads, size = queries.shape
    slots = keys.shape[2]
    share = out.shape[1]
    blocks = n_seq * n_kvh

    step = rows // 4
    loads = {
        "lengths": pltpu.make_async_copy(lengths, l_buf, load_sem.at[0]),
        "queries": pltpu.make_async_copy(queries, q_buf, load_sem.at[1]),
    }
    for n in range(4):
        some = pl.ds(n * step, step)
        loads["keys", n * step] = pltpu.make_async_copy(
            keys.at[some], k_buf.at[some], load_sem.at[2 + n]
        )
    for n in range(4):
        some = pl.ds(n * step, step)
        loads["values", n * step] = pltpu.make_async_copy(
            values.at[some], v_buf.at[some], load_sem.at[6 + n]
        )
    loads["weights"] = pltpu.make_async_copy(weights.at[0, 0], w_buf, load_sem.at[10])
    loads["residual"] = pltpu.make_async_copy(residual, r_buf, load_sem.at[11])
    for load in loads.values():
        load.start()

    seq_peers = [partner(seq, i, n_seq) for i in range(n_seq)]
    kvh_peers = [partner(kvh, j, n_kvh) for j in range(n_kvh)]
    barrier = pltpu.get_barrier_semaphore()
    greeted = 0
    for i in range(n_seq):
        for j in range(n_kvh):
            if (i or j) and (cut or not (i and j)):
                target = {"seq": seq_peers[i], "kvh": kvh_peers[j]}
                pl.semaphore_signal(barrier, inc=1, device_id=target, device_id_type=MESH)
                greeted += 1

    row = lax.broadcasted_iota(jnp.int32, (rows, slots), 0)
    slot = lax.broadcasted_iota(jnp.int32, (rows, slots), 1)
    length = jnp.zeros((rows, slots), jnp.int32)
    loads["lengths"].wait()
    for b in range(rows):
        length = jnp.where(row == b, l_buf[b], length)
    position = (slot // BLOCK_POSITIONS * n_seq + seq) * BLOCK_POSITIONS + slot % BLOCK_POSITIONS
    live = position < length
    out_row = lax.broadcasted_iota(jnp.int32, (rows, size), 0)

    loads["queries"].wait()
    for b in range(rows):
        q_rows[pl.ds(b * heads, heads), :] = q_buf[b, 0].astype(jnp.float32)
    q = jnp.concatenate(
        [q_rows[pl.ds(g, rows, stride=heads), :] for g in range(heads)], axis=0
    ).astype(jnp.bfloat16)

    scores = jnp.zeros((heads, rows, slots), jnp.float32)
    for b in range(rows):
        if b % step == 0:
            loads["keys", b].wait()
        full = lax.dot_general(
            q, k_buf[b, 0], (((1,), (1,)), ((), ())), preferred_element_type=jnp.float32
        ).reshape(heads, rows, slots)
        scores = jnp.where((row == b)[None], full, scores)
    scores = jnp.where(live[None], scores * (1.0 / math.sqrt(size)), -1e30)
    top = jnp.max(scores, axis=2, keepdims=True)
    probs = jnp.exp(scores - top)
    total = jnp.sum(probs, axis=2, keepdims=True)
    probs = probs.reshape(heads * rows, slots).astype(jnp.bfloat16)
    summed = jnp.zeros((heads, rows, size), jnp.float32)
    for b in range(rows):
        if b % step == 0:
            loads["values", b].wait()
        full = jnp.dot(probs, v_buf[b, 0], preferred_element_type=jnp.float32)
        summed = jnp.where((out_row == b)[None], full.reshape(heads, rows, size), summed)
    part_send[:, :rows, :] = summed / total
    part_send[:, rows:, :] = jnp.broadcast_to(top + jnp.log(total), (heads, rows, size))

    pl.semaphore_wait(barrier, greeted)
    sends = []
    order = list(range(n_seq - 1, 0, -1))
    part_copies = {}
    for i in order:
        copy = pltpu.make_async_remote_copy(
            src_ref=part_send.at[seq_peers[i]],
            dst_ref=part_recv.at[i],
            send_sem=ps_sem.at[i],
            recv_sem=pr_sem.at[i],
            device_id={"seq": seq_peers[i]},
            device_id_type=MESH,
        )
        copy.start()
        part_copies[i] = copy
        sends.append(copy)

    loads["weights"].wait()
    loads["residual"].wait()
    parts = [part_send[seq]]
    for i in range(1, n_seq):
        part_copies[i].wait_recv()
        parts.append(part_recv[i])
    highest = functools.reduce(jnp.maximum, [part[rows:] for part in parts])
    factors = [jnp.exp(part[rows:] - highest) for part in parts]
    joined = sum(factor * part[:rows] for factor, part in zip(factors, parts))
    attended = (joined / sum(factors)).astype(jnp.bfloat16)

    aligned = share % 128 == 0
    if not aligned:
        for first in range(0, blocks * share, 1024):
            tile = jnp.dot(
                attended, w_buf[:, first:first + 1024], preferred_element_type=jnp.float32
            )
            for block in range(1024 // share):
                contrib[first // share + block] = tile[:, block * share:(block + 1) * share]

    def contribution(i, j, first, count):
        block = seq_peers[i] * n_kvh + kvh_peers[j]
        if not aligned:
            return contrib[block]
        columns = pl.ds(pl.multiple_of(block * share + first, 128), count)
        return jnp.dot(attended, w_buf[:, columns], preferred_element_type=jnp.float32)

    order.append(0)
    low, high = pl.ds(0, cut), pl.ds(cut, share - cut)
    direct_copies = {}
    core_copies = {}
    for i in order:
        for j in range(n_kvh):
            if i and cut:
                direct_send[i, j] = contribution(i, j, 0, cut)
                target = {"seq": seq_peers[i]}
                if j:
                    target["kvh"] = kvh_peers[j]
                copy = pltpu.make_async_remote_copy(
                    src_ref=direct_send.at[i, j],
                    dst_ref=direct_recv.at[i, j],
                    send_sem=ds_sem.at[i, j],
                    recv_sem=dr_sem.at[i, j],
                    device_id=target,
                    device_id_type=MESH,
                )
                copy.start()
                direct_copies[i, j] = copy
                sends.append(copy)
        for j in range(1, n_kvh):
            first = cut if i else 0
            if first < share:
                part = pl.ds(first, share - first)
                core_send[i, j, :, part] = contribution(i, j, first, share - first)
                copy = pltpu.make_async_remote_copy(
                    src_ref=core_send.at[i, j, :, part],
                    dst_ref=core_recv.at[i, j, :, part],
                    send_sem=cs_sem.at[i, j],
                    recv_sem=cr_sem.at[i, j],
                    device_id={"kvh": kvh_peers[j]},
                    device_id_type=MESH,
                )
                copy.start()
                core_copies[i, j] = copy
                sends.append(copy)
    seq_copies = {}
    if cut < share:
        waiting = order[:-1]
        seq_send[waiting[0], :, high] = contribution(waiting[0], 0, cut, share - cut)
        for i, after in zip(waiting, waiting[1:] + [None]):
            if after is not None:
                seq_send[after, :, high] = contribution(after, 0, cut, share - cut)
            own = seq_send[i, :, high]
            for j in range(1, n_kvh):
                core_copies[i, j].wait_recv()
                own = own + core_recv[i, j, :, high]
            seq_send[i, :, high] = own
            copy = pltpu.make_async_remote_copy(
                src_ref=seq_send.at[i, :, high],
                dst_ref=seq_recv.at[i, :, high],
                send_sem=ss_sem.at[i],
                recv_sem=sr_sem.at[i],
                device_id={"seq": seq_peers[i]},
                device_id_type=MESH,
            )
            copy.start()
            seq_copies[i] = copy
            sends.append(copy)
    result = r_buf[...] + contribution(0, 0, 0, share)
    for j in range(1, n_kvh):
        core_copies[0, j].wait_recv()
        result = result + core_recv[0, j]
    out[...] = result
    if cut:
        result = out[:, low]
        for i in order[:-1][::-1]:
            for j in range(n_kvh):
                direct_copies[i, j].wait_recv()
                result = result + direct_recv[i, j]
        out[:, low] = result
    if cut < share:
        result = out[:, high]
        for i in order[:-1][::-1]:
            seq_copies[i].wait_recv()
            result = result + seq_recv[i, :, high]
        out[:, high] = result
    for copy in sends:
        copy.wait_send()


def body(n_seq, n_kvh, queries, keys, values, lengths, weights, residual):
    rows, _, heads, size = queries.shape
    slots = keys.shape[2]
    features = weights.shape[3]
    share = residual.shape[1]
    cut = min(DIRECT_COLUMNS, share) if share % 128 == 0 else 0
    f32, bf16 = jnp.float32, jnp.bfloat16
    dma = pltpu.SemaphoreType.DMA
    in_hbm = pl.BlockSpec(memory_space=pltpu.HBM)
    return pl.pallas_call(
        functools.partial(kernel, n_seq, n_kvh, cut),
        out_shape=jax.ShapeDtypeStruct((rows, share), f32),
        in_specs=[in_hbm] * 6,
        out_specs=pl.BlockSpec(memory_space=pltpu.VMEM),
        scratch_shapes=[
            pltpu.SMEM((rows,), jnp.int32),
            pltpu.VMEM((rows, 1, heads, size), bf16),
            pltpu.VMEM((rows * heads, size), f32),
            pltpu.VMEM((rows, 1, slots, size), bf16),
            pltpu.VMEM((rows, 1, slots, size), bf16),
            pltpu.VMEM((size, features), bf16),
            pltpu.VMEM((rows, share), f32),
            pltpu.VMEM((heads, 2 * rows, size), f32),
            pltpu.VMEM((n_seq, 2 * rows, size), f32),
            pltpu.VMEM((n_seq, n_kvh, rows, max(cut, 128)), f32),
            pltpu.VMEM((n_seq, n_kvh, rows, max(cut, 128)), f32),
            pltpu.VMEM((n_seq, n_kvh, rows, share), f32),
            pltpu.VMEM((n_seq, n_kvh, rows, share), f32),
            pltpu.VMEM((n_seq, rows, share), f32),
            pltpu.VMEM((n_seq, rows, share), f32),
            pltpu.VMEM((n_seq * n_kvh if share % 128 else 1, rows, share), f32),
            dma((12,)),
            dma((n_seq,)),
            dma((n_seq,)),
            dma((n_seq, n_kvh)),
            dma((n_seq, n_kvh)),
            dma((n_seq, n_kvh)),
            dma((n_seq, n_kvh)),
            dma((n_seq,)),
            dma((n_seq,)),
        ],
        compiler_params=pltpu.CompilerParams(
            collective_id=0, has_side_effects=True, vmem_limit_bytes=40 * 1024 * 1024
        ),
        cost_estimate=pl.CostEstimate(
            flops=2 * rows * size * features, bytes_accessed=2 * size * features, transcendentals=0
        ),
    )(*[
        pltpu.with_memory_space_constraint(array, pltpu.HBM)
        for array in (lengths, queries, keys, values, weights, residual)
    ])


def solution(mesh):
    in_specs = (
        P("rep", "kvh", None, None),
        P("rep", "kvh", "seq", None),
        P("rep", "kvh", "seq", None),
        P("rep"),
        P("kvh", "seq", None, None),
        P("rep", ("seq", "kvh")),
    )
    out_specs = P("rep", ("seq", "kvh"))
    run = functools.partial(body, mesh.shape["seq"], mesh.shape["kvh"])
    return jax.shard_map(run, mesh=mesh, in_specs=in_specs, out_specs=out_specs, check_vma=False)
```

```python
import functools
import math

import jax
import jax.numpy as jnp
from jax import lax
from jax.experimental import pallas as pl
from jax.experimental.pallas import tpu as pltpu
from jax.sharding import PartitionSpec as P

BLOCK_POSITIONS = 32
DIRECT_COLUMNS = 0
MESH = pl.DeviceIdType.MESH


def partner(me, step, count):
    result = 0
    bit = 1
    while bit < count:
        own = lax.rem(lax.div(me, bit), 2)
        result = result + bit * (1 - own if (step // bit) % 2 else own)
        bit *= 2
    return result


def kernel(
    n_seq, n_kvh, cut,
    lengths, queries, keys, values, weights, residual, out,
    l_buf, q_buf, q_rows, k_buf, v_buf, w_buf, r_buf,
    part_send, part_recv, direct_send, direct_recv, core_send, core_recv,
    seq_send, seq_recv, contrib,
    load_sem, ps_sem, pr_sem, ds_sem, dr_sem, cs_sem, cr_sem, ss_sem, sr_sem,
):
    seq = lax.axis_index("seq")
    kvh = lax.axis_index("kvh")
    rows, _, heads, size = queries.shape
    slots = keys.shape[2]
    share = out.shape[1]
    blocks = n_seq * n_kvh

    loads = {
        "keys": pltpu.make_async_copy(keys, k_buf, load_sem.at[0]),
        "queries": pltpu.make_async_copy(queries, q_buf, load_sem.at[1]),
        "lengths": pltpu.make_async_copy(lengths, l_buf, load_sem.at[2]),
        "values": pltpu.make_async_copy(values, v_buf, load_sem.at[3]),
        "weights": pltpu.make_async_copy(weights.at[0, 0], w_buf, load_sem.at[4]),
        "residual": pltpu.make_async_copy(residual, r_buf, load_sem.at[5]),
    }
    for name in ("keys", "queries", "lengths", "values"):
        loads[name].start()

    seq_peers = [partner(seq, i, n_seq) for i in range(n_seq)]
    kvh_peers = [partner(kvh, j, n_kvh) for j in range(n_kvh)]
    barrier = pltpu.get_barrier_semaphore()
    greeted = 0
    for i in range(n_seq):
        for j in range(n_kvh):
            if (i or j) and (cut or not (i and j)):
                target = {"seq": seq_peers[i], "kvh": kvh_peers[j]}
                pl.semaphore_signal(barrier, inc=1, device_id=target, device_id_type=MESH)
                greeted += 1

    row = lax.broadcasted_iota(jnp.int32, (rows, slots), 0)
    slot = lax.broadcasted_iota(jnp.int32, (rows, slots), 1)
    length = jnp.zeros((rows, slots), jnp.int32)
    loads["lengths"].wait()
    for b in range(rows):
        length = jnp.where(row == b, l_buf[b], length)
    position = (slot // BLOCK_POSITIONS * n_seq + seq) * BLOCK_POSITIONS + slot % BLOCK_POSITIONS
    live = position < length
    out_row = lax.broadcasted_iota(jnp.int32, (rows, size), 0)

    loads["queries"].wait()
    for b in range(rows):
        q_rows[pl.ds(b * heads, heads), :] = q_buf[b, 0].astype(jnp.float32)
    q = jnp.concatenate(
        [q_rows[pl.ds(g, rows, stride=heads), :] for g in range(heads)], axis=0
    ).astype(jnp.bfloat16)

    loads["keys"].wait()
    loads["weights"].start()
    loads["residual"].start()
    scores = jnp.zeros((heads, rows, slots), jnp.float32)
    for b in range(rows):
        full = lax.dot_general(
            q, k_buf[b, 0], (((1,), (1,)), ((), ())), preferred_element_type=jnp.float32
        ).reshape(heads, rows, slots)
        scores = jnp.where((row == b)[None], full, scores)
    scores = jnp.where(live[None], scores * (1.0 / math.sqrt(size)), -1e30)
    top = jnp.max(scores, axis=2, keepdims=True)
    probs = jnp.exp(scores - top)
    total = jnp.sum(probs, axis=2, keepdims=True)
    probs = probs.reshape(heads * rows, slots).astype(jnp.bfloat16)
    loads["values"].wait()
    summed = jnp.zeros((heads, rows, size), jnp.float32)
    for b in range(rows):
        full = jnp.dot(probs, v_buf[b, 0], preferred_element_type=jnp.float32)
        summed = jnp.where((out_row == b)[None], full.reshape(heads, rows, size), summed)
    part_send[:, :rows, :] = summed / total
    part_send[:, rows:, :] = jnp.broadcast_to(top + jnp.log(total), (heads, rows, size))

    pl.semaphore_wait(barrier, greeted)
    sends = []
    order = list(range(n_seq - 1, 0, -1))
    part_copies = {}
    for i in order:
        copy = pltpu.make_async_remote_copy(
            src_ref=part_send.at[seq_peers[i]],
            dst_ref=part_recv.at[i],
            send_sem=ps_sem.at[i],
            recv_sem=pr_sem.at[i],
            device_id={"seq": seq_peers[i]},
            device_id_type=MESH,
        )
        copy.start()
        part_copies[i] = copy
        sends.append(copy)

    loads["weights"].wait()
    loads["residual"].wait()
    parts = [part_send[seq]]
    for i in range(1, n_seq):
        part_copies[i].wait_recv()
        parts.append(part_recv[i])
    highest = functools.reduce(jnp.maximum, [part[rows:] for part in parts])
    factors = [jnp.exp(part[rows:] - highest) for part in parts]
    joined = sum(factor * part[:rows] for factor, part in zip(factors, parts))
    attended = (joined / sum(factors)).astype(jnp.bfloat16)

    aligned = share % 128 == 0
    if not aligned:
        for first in range(0, blocks * share, 1024):
            tile = jnp.dot(
                attended, w_buf[:, first:first + 1024], preferred_element_type=jnp.float32
            )
            for block in range(1024 // share):
                contrib[first // share + block] = tile[:, block * share:(block + 1) * share]

    def contribution(i, j, first, count):
        block = seq_peers[i] * n_kvh + kvh_peers[j]
        if not aligned:
            return contrib[block]
        columns = pl.ds(pl.multiple_of(block * share + first, 128), count)
        return jnp.dot(attended, w_buf[:, columns], preferred_element_type=jnp.float32)

    order.append(0)
    low, high = pl.ds(0, cut), pl.ds(cut, share - cut)
    direct_copies = {}
    core_copies = {}
    for i in order:
        for j in range(n_kvh):
            if i and cut:
                direct_send[i, j] = contribution(i, j, 0, cut)
                target = {"seq": seq_peers[i]}
                if j:
                    target["kvh"] = kvh_peers[j]
                copy = pltpu.make_async_remote_copy(
                    src_ref=direct_send.at[i, j],
                    dst_ref=direct_recv.at[i, j],
                    send_sem=ds_sem.at[i, j],
                    recv_sem=dr_sem.at[i, j],
                    device_id=target,
                    device_id_type=MESH,
                )
                copy.start()
                direct_copies[i, j] = copy
                sends.append(copy)
        for j in range(1, n_kvh):
            first = cut if i else 0
            if first < share:
                part = pl.ds(first, share - first)
                core_send[i, j, :, part] = contribution(i, j, first, share - first)
                copy = pltpu.make_async_remote_copy(
                    src_ref=core_send.at[i, j, :, part],
                    dst_ref=core_recv.at[i, j, :, part],
                    send_sem=cs_sem.at[i, j],
                    recv_sem=cr_sem.at[i, j],
                    device_id={"kvh": kvh_peers[j]},
                    device_id_type=MESH,
                )
                copy.start()
                core_copies[i, j] = copy
                sends.append(copy)
    seq_copies = {}
    if cut < share:
        waiting = order[:-1]
        seq_send[waiting[0], :, high] = contribution(waiting[0], 0, cut, share - cut)
        for i, after in zip(waiting, waiting[1:] + [None]):
            if after is not None:
                seq_send[after, :, high] = contribution(after, 0, cut, share - cut)
            own = seq_send[i, :, high]
            for j in range(1, n_kvh):
                core_copies[i, j].wait_recv()
                own = own + core_recv[i, j, :, high]
            seq_send[i, :, high] = own
            copy = pltpu.make_async_remote_copy(
                src_ref=seq_send.at[i, :, high],
                dst_ref=seq_recv.at[i, :, high],
                send_sem=ss_sem.at[i],
                recv_sem=sr_sem.at[i],
                device_id={"seq": seq_peers[i]},
                device_id_type=MESH,
            )
            copy.start()
            seq_copies[i] = copy
            sends.append(copy)
    result = r_buf[...] + contribution(0, 0, 0, share)
    for j in range(1, n_kvh):
        core_copies[0, j].wait_recv()
        result = result + core_recv[0, j]
    out[...] = result
    if cut:
        result = out[:, low]
        for i in order[:-1][::-1]:
            for j in range(n_kvh):
                direct_copies[i, j].wait_recv()
                result = result + direct_recv[i, j]
        out[:, low] = result
    if cut < share:
        result = out[:, high]
        for i in order[:-1][::-1]:
            seq_copies[i].wait_recv()
            result = result + seq_recv[i, :, high]
        out[:, high] = result
    for copy in sends:
        copy.wait_send()


def body(n_seq, n_kvh, queries, keys, values, lengths, weights, residual):
    rows, _, heads, size = queries.shape
    slots = keys.shape[2]
    features = weights.shape[3]
    share = residual.shape[1]
    cut = min(DIRECT_COLUMNS, share) if share % 128 == 0 else 0
    f32, bf16 = jnp.float32, jnp.bfloat16
    dma = pltpu.SemaphoreType.DMA
    in_hbm = pl.BlockSpec(memory_space=pltpu.HBM)
    return pl.pallas_call(
        functools.partial(kernel, n_seq, n_kvh, cut),
        out_shape=jax.ShapeDtypeStruct((rows, share), f32),
        in_specs=[in_hbm] * 6,
        out_specs=pl.BlockSpec(memory_space=pltpu.VMEM),
        scratch_shapes=[
            pltpu.SMEM((rows,), jnp.int32),
            pltpu.VMEM((rows, 1, heads, size), bf16),
            pltpu.VMEM((rows * heads, size), f32),
            pltpu.VMEM((rows, 1, slots, size), bf16),
            pltpu.VMEM((rows, 1, slots, size), bf16),
            pltpu.VMEM((size, features), bf16),
            pltpu.VMEM((rows, share), f32),
            pltpu.VMEM((heads, 2 * rows, size), f32),
            pltpu.VMEM((n_seq, 2 * rows, size), f32),
            pltpu.VMEM((n_seq, n_kvh, rows, max(cut, 128)), f32),
            pltpu.VMEM((n_seq, n_kvh, rows, max(cut, 128)), f32),
            pltpu.VMEM((n_seq, n_kvh, rows, share), f32),
            pltpu.VMEM((n_seq, n_kvh, rows, share), f32),
            pltpu.VMEM((n_seq, rows, share), f32),
            pltpu.VMEM((n_seq, rows, share), f32),
            pltpu.VMEM((n_seq * n_kvh if share % 128 else 1, rows, share), f32),
            dma((6,)),
            dma((n_seq,)),
            dma((n_seq,)),
            dma((n_seq, n_kvh)),
            dma((n_seq, n_kvh)),
            dma((n_seq, n_kvh)),
            dma((n_seq, n_kvh)),
            dma((n_seq,)),
            dma((n_seq,)),
        ],
        compiler_params=pltpu.CompilerParams(
            collective_id=0, has_side_effects=True, vmem_limit_bytes=40 * 1024 * 1024
        ),
        cost_estimate=pl.CostEstimate(
            flops=2 * rows * size * features, bytes_accessed=2 * size * features, transcendentals=0
        ),
    )(*[
        pltpu.with_memory_space_constraint(array, pltpu.HBM)
        for array in (lengths, queries, keys, values, weights, residual)
    ])


def solution(mesh):
    in_specs = (
        P("rep", "kvh", None, None),
        P("rep", "kvh", "seq", None),
        P("rep", "kvh", "seq", None),
        P("rep"),
        P("kvh", "seq", None, None),
        P("rep", ("seq", "kvh")),
    )
    out_specs = P("rep", ("seq", "kvh"))
    run = functools.partial(body, mesh.shape["seq"], mesh.shape["kvh"])
    return jax.shard_map(run, mesh=mesh, in_specs=in_specs, out_specs=out_specs, check_vma=False)
```

```python
import functools
import math

import jax
import jax.numpy as jnp
from jax import lax
from jax.experimental import pallas as pl
from jax.experimental.pallas import tpu as pltpu
from jax.sharding import PartitionSpec as P

BLOCK_POSITIONS = 32
DIRECT_COLUMNS = 1024
MESH = pl.DeviceIdType.MESH


def partner(me, step, count):
    result = 0
    bit = 1
    while bit < count:
        own = lax.rem(lax.div(me, bit), 2)
        result = result + bit * (1 - own if (step // bit) % 2 else own)
        bit *= 2
    return result


def kernel(
    n_seq, n_kvh, cut,
    lengths, queries, keys, values, weights, residual, out,
    l_buf, q_buf, q_rows, k_buf, v_buf, w_buf, r_buf,
    part_send, part_recv, direct_send, direct_recv, core_send, core_recv,
    seq_send, seq_recv, contrib,
    load_sem, ps_sem, pr_sem, ds_sem, dr_sem, cs_sem, cr_sem, ss_sem, sr_sem,
):
    seq = lax.axis_index("seq")
    kvh = lax.axis_index("kvh")
    rows, _, heads, size = queries.shape
    slots = keys.shape[2]
    share = out.shape[1]
    blocks = n_seq * n_kvh

    loads = {
        "keys": pltpu.make_async_copy(keys, k_buf, load_sem.at[0]),
        "queries": pltpu.make_async_copy(queries, q_buf, load_sem.at[1]),
        "lengths": pltpu.make_async_copy(lengths, l_buf, load_sem.at[2]),
        "values": pltpu.make_async_copy(values, v_buf, load_sem.at[3]),
        "weights": pltpu.make_async_copy(weights.at[0, 0], w_buf, load_sem.at[4]),
        "residual": pltpu.make_async_copy(residual, r_buf, load_sem.at[5]),
    }
    for name in ("keys", "queries", "lengths", "values"):
        loads[name].start()

    seq_peers = [partner(seq, i, n_seq) for i in range(n_seq)]
    kvh_peers = [partner(kvh, j, n_kvh) for j in range(n_kvh)]
    barrier = pltpu.get_barrier_semaphore()
    greeted = 0
    for i in range(n_seq):
        for j in range(n_kvh):
            if (i or j) and (cut or not (i and j)):
                target = {"seq": seq_peers[i], "kvh": kvh_peers[j]}
                pl.semaphore_signal(barrier, inc=1, device_id=target, device_id_type=MESH)
                greeted += 1

    row = lax.broadcasted_iota(jnp.int32, (rows, slots), 0)
    slot = lax.broadcasted_iota(jnp.int32, (rows, slots), 1)
    length = jnp.zeros((rows, slots), jnp.int32)
    loads["lengths"].wait()
    for b in range(rows):
        length = jnp.where(row == b, l_buf[b], length)
    position = (slot // BLOCK_POSITIONS * n_seq + seq) * BLOCK_POSITIONS + slot % BLOCK_POSITIONS
    live = position < length
    out_row = lax.broadcasted_iota(jnp.int32, (rows, size), 0)

    loads["queries"].wait()
    for b in range(rows):
        q_rows[pl.ds(b * heads, heads), :] = q_buf[b, 0].astype(jnp.float32)
    q = jnp.concatenate(
        [q_rows[pl.ds(g, rows, stride=heads), :] for g in range(heads)], axis=0
    ).astype(jnp.bfloat16)

    loads["keys"].wait()
    loads["weights"].start()
    loads["residual"].start()
    scores = jnp.zeros((heads, rows, slots), jnp.float32)
    for b in range(rows):
        full = lax.dot_general(
            q, k_buf[b, 0], (((1,), (1,)), ((), ())), preferred_element_type=jnp.float32
        ).reshape(heads, rows, slots)
        scores = jnp.where((row == b)[None], full, scores)
    scores = jnp.where(live[None], scores * (1.0 / math.sqrt(size)), -1e30)
    top = jnp.max(scores, axis=2, keepdims=True)
    probs = jnp.exp(scores - top)
    total = jnp.sum(probs, axis=2, keepdims=True)
    probs = probs.reshape(heads * rows, slots).astype(jnp.bfloat16)
    loads["values"].wait()
    summed = jnp.zeros((heads, rows, size), jnp.float32)
    for b in range(rows):
        full = jnp.dot(probs, v_buf[b, 0], preferred_element_type=jnp.float32)
        summed = jnp.where((out_row == b)[None], full.reshape(heads, rows, size), summed)
    part_send[:, :rows, :] = summed / total
    part_send[:, rows:, :] = jnp.broadcast_to(top + jnp.log(total), (heads, rows, size))

    pl.semaphore_wait(barrier, greeted)
    sends = []
    order = list(range(n_seq - 1, 0, -1))
    part_copies = {}
    for i in order:
        copy = pltpu.make_async_remote_copy(
            src_ref=part_send.at[seq_peers[i]],
            dst_ref=part_recv.at[i],
            send_sem=ps_sem.at[i],
            recv_sem=pr_sem.at[i],
            device_id={"seq": seq_peers[i]},
            device_id_type=MESH,
        )
        copy.start()
        part_copies[i] = copy
        sends.append(copy)

    loads["weights"].wait()
    loads["residual"].wait()
    parts = [part_send[seq]]
    for i in range(1, n_seq):
        part_copies[i].wait_recv()
        parts.append(part_recv[i])
    highest = functools.reduce(jnp.maximum, [part[rows:] for part in parts])
    factors = [jnp.exp(part[rows:] - highest) for part in parts]
    joined = sum(factor * part[:rows] for factor, part in zip(factors, parts))
    attended = (joined / sum(factors)).astype(jnp.bfloat16)

    aligned = share % 128 == 0
    if not aligned:
        for first in range(0, blocks * share, 1024):
            tile = jnp.dot(
                attended, w_buf[:, first:first + 1024], preferred_element_type=jnp.float32
            )
            for block in range(1024 // share):
                contrib[first // share + block] = tile[:, block * share:(block + 1) * share]

    def contribution(i, j, first, count):
        block = seq_peers[i] * n_kvh + kvh_peers[j]
        if not aligned:
            return contrib[block]
        columns = pl.ds(pl.multiple_of(block * share + first, 128), count)
        return jnp.dot(attended, w_buf[:, columns], preferred_element_type=jnp.float32)

    order.append(0)
    low, high = pl.ds(0, cut), pl.ds(cut, share - cut)
    direct_copies = {}
    core_copies = {}
    for i in order:
        for j in range(n_kvh):
            if i and cut:
                direct_send[i, j] = contribution(i, j, 0, cut)
                target = {"seq": seq_peers[i]}
                if j:
                    target["kvh"] = kvh_peers[j]
                copy = pltpu.make_async_remote_copy(
                    src_ref=direct_send.at[i, j],
                    dst_ref=direct_recv.at[i, j],
                    send_sem=ds_sem.at[i, j],
                    recv_sem=dr_sem.at[i, j],
                    device_id=target,
                    device_id_type=MESH,
                )
                copy.start()
                direct_copies[i, j] = copy
                sends.append(copy)
        for j in range(1, n_kvh):
            first = cut if i else 0
            if first < share:
                part = pl.ds(first, share - first)
                core_send[i, j, :, part] = contribution(i, j, first, share - first)
                copy = pltpu.make_async_remote_copy(
                    src_ref=core_send.at[i, j, :, part],
                    dst_ref=core_recv.at[i, j, :, part],
                    send_sem=cs_sem.at[i, j],
                    recv_sem=cr_sem.at[i, j],
                    device_id={"kvh": kvh_peers[j]},
                    device_id_type=MESH,
                )
                copy.start()
                core_copies[i, j] = copy
                sends.append(copy)
    seq_copies = {}
    if cut < share:
        waiting = order[:-1]
        seq_send[waiting[0], :, high] = contribution(waiting[0], 0, cut, share - cut)
        for i, after in zip(waiting, waiting[1:] + [None]):
            if after is not None:
                seq_send[after, :, high] = contribution(after, 0, cut, share - cut)
            own = seq_send[i, :, high]
            for j in range(1, n_kvh):
                core_copies[i, j].wait_recv()
                own = own + core_recv[i, j, :, high]
            seq_send[i, :, high] = own
            copy = pltpu.make_async_remote_copy(
                src_ref=seq_send.at[i, :, high],
                dst_ref=seq_recv.at[i, :, high],
                send_sem=ss_sem.at[i],
                recv_sem=sr_sem.at[i],
                device_id={"seq": seq_peers[i]},
                device_id_type=MESH,
            )
            copy.start()
            seq_copies[i] = copy
            sends.append(copy)
    result = r_buf[...] + contribution(0, 0, 0, share)
    for j in range(1, n_kvh):
        core_copies[0, j].wait_recv()
        result = result + core_recv[0, j]
    out[...] = result
    if cut:
        result = out[:, low]
        for i in order[:-1][::-1]:
            for j in range(n_kvh):
                direct_copies[i, j].wait_recv()
                result = result + direct_recv[i, j]
        out[:, low] = result
    if cut < share:
        result = out[:, high]
        for i in order[:-1][::-1]:
            seq_copies[i].wait_recv()
            result = result + seq_recv[i, :, high]
        out[:, high] = result
    for copy in sends:
        copy.wait_send()


def body(n_seq, n_kvh, queries, keys, values, lengths, weights, residual):
    rows, _, heads, size = queries.shape
    slots = keys.shape[2]
    features = weights.shape[3]
    share = residual.shape[1]
    cut = min(DIRECT_COLUMNS, share) if share % 128 == 0 else 0
    f32, bf16 = jnp.float32, jnp.bfloat16
    dma = pltpu.SemaphoreType.DMA
    in_hbm = pl.BlockSpec(memory_space=pltpu.HBM)
    return pl.pallas_call(
        functools.partial(kernel, n_seq, n_kvh, cut),
        out_shape=jax.ShapeDtypeStruct((rows, share), f32),
        in_specs=[in_hbm] * 6,
        out_specs=pl.BlockSpec(memory_space=pltpu.VMEM),
        scratch_shapes=[
            pltpu.SMEM((rows,), jnp.int32),
            pltpu.VMEM((rows, 1, heads, size), bf16),
            pltpu.VMEM((rows * heads, size), f32),
            pltpu.VMEM((rows, 1, slots, size), bf16),
            pltpu.VMEM((rows, 1, slots, size), bf16),
            pltpu.VMEM((size, features), bf16),
            pltpu.VMEM((rows, share), f32),
            pltpu.VMEM((heads, 2 * rows, size), f32),
            pltpu.VMEM((n_seq, 2 * rows, size), f32),
            pltpu.VMEM((n_seq, n_kvh, rows, max(cut, 128)), f32),
            pltpu.VMEM((n_seq, n_kvh, rows, max(cut, 128)), f32),
            pltpu.VMEM((n_seq, n_kvh, rows, share), f32),
            pltpu.VMEM((n_seq, n_kvh, rows, share), f32),
            pltpu.VMEM((n_seq, rows, share), f32),
            pltpu.VMEM((n_seq, rows, share), f32),
            pltpu.VMEM((n_seq * n_kvh if share % 128 else 1, rows, share), f32),
            dma((6,)),
            dma((n_seq,)),
            dma((n_seq,)),
            dma((n_seq, n_kvh)),
            dma((n_seq, n_kvh)),
            dma((n_seq, n_kvh)),
            dma((n_seq, n_kvh)),
            dma((n_seq,)),
            dma((n_seq,)),
        ],
        compiler_params=pltpu.CompilerParams(
            collective_id=0, has_side_effects=True, vmem_limit_bytes=40 * 1024 * 1024
        ),
        cost_estimate=pl.CostEstimate(
            flops=2 * rows * size * features, bytes_accessed=2 * size * features, transcendentals=0
        ),
    )(*[
        pltpu.with_memory_space_constraint(array, pltpu.HBM)
        for array in (lengths, queries, keys, values, weights, residual)
    ])


def solution(mesh):
    in_specs = (
        P("rep", "kvh", None, None),
        P("rep", "kvh", "seq", None),
        P("rep", "kvh", "seq", None),
        P("rep"),
        P("kvh", "seq", None, None),
        P("rep", ("seq", "kvh")),
    )
    out_specs = P("rep", ("seq", "kvh"))
    run = functools.partial(body, mesh.shape["seq"], mesh.shape["kvh"])
    return jax.shard_map(run, mesh=mesh, in_specs=in_specs, out_specs=out_specs, check_vma=False)
```

```python
import functools
import math

import jax
import jax.numpy as jnp
from jax import lax
from jax.experimental import pallas as pl
from jax.experimental.pallas import tpu as pltpu
from jax.sharding import PartitionSpec as P

BLOCK_POSITIONS = 32
DIRECT_COLUMNS = 1024
MESH = pl.DeviceIdType.MESH


def partner(me, step, count):
    result = 0
    bit = 1
    while bit < count:
        own = lax.rem(lax.div(me, bit), 2)
        result = result + bit * (1 - own if (step // bit) % 2 else own)
        bit *= 2
    return result


def kernel(
    n_seq, n_kvh, cut,
    lengths, queries, keys, values, weights, residual, out,
    l_buf, q_buf, q_rows, k_buf, v_buf, w_buf, r_buf,
    part_send, part_recv, direct_send, direct_recv, core_send, core_recv,
    seq_send, seq_recv, contrib,
    load_sem, ps_sem, pr_sem, ds_sem, dr_sem, cs_sem, cr_sem, ss_sem, sr_sem,
):
    seq = lax.axis_index("seq")
    kvh = lax.axis_index("kvh")
    rows, _, heads, size = queries.shape
    slots = keys.shape[2]
    share = out.shape[1]
    blocks = n_seq * n_kvh

    loads = {
        "keys": pltpu.make_async_copy(keys, k_buf, load_sem.at[0]),
        "queries": pltpu.make_async_copy(queries, q_buf, load_sem.at[1]),
        "lengths": pltpu.make_async_copy(lengths, l_buf, load_sem.at[2]),
        "values": pltpu.make_async_copy(values, v_buf, load_sem.at[3]),
        "weights": pltpu.make_async_copy(weights.at[0, 0], w_buf, load_sem.at[4]),
        "residual": pltpu.make_async_copy(residual, r_buf, load_sem.at[5]),
    }
    for load in loads.values():
        load.start()

    seq_peers = [partner(seq, i, n_seq) for i in range(n_seq)]
    kvh_peers = [partner(kvh, j, n_kvh) for j in range(n_kvh)]
    barrier = pltpu.get_barrier_semaphore()
    greeted = 0
    for i in range(n_seq):
        for j in range(n_kvh):
            if (i or j) and (cut or not (i and j)):
                target = {"seq": seq_peers[i], "kvh": kvh_peers[j]}
                pl.semaphore_signal(barrier, inc=1, device_id=target, device_id_type=MESH)
                greeted += 1

    row = lax.broadcasted_iota(jnp.int32, (rows, slots), 0)
    slot = lax.broadcasted_iota(jnp.int32, (rows, slots), 1)
    length = jnp.zeros((rows, slots), jnp.int32)
    loads["lengths"].wait()
    for b in range(rows):
        length = jnp.where(row == b, l_buf[b], length)
    position = (slot // BLOCK_POSITIONS * n_seq + seq) * BLOCK_POSITIONS + slot % BLOCK_POSITIONS
    live = position < length
    out_row = lax.broadcasted_iota(jnp.int32, (rows, size), 0)

    loads["queries"].wait()
    for b in range(rows):
        q_rows[pl.ds(b * heads, heads), :] = q_buf[b, 0].astype(jnp.float32)
    q = jnp.concatenate(
        [q_rows[pl.ds(g, rows, stride=heads), :] for g in range(heads)], axis=0
    ).astype(jnp.bfloat16)

    loads["keys"].wait()
    scores = jnp.zeros((heads, rows, slots), jnp.float32)
    for b in range(rows):
        full = lax.dot_general(
            q, k_buf[b, 0], (((1,), (1,)), ((), ())), preferred_element_type=jnp.float32
        ).reshape(heads, rows, slots)
        scores = jnp.where((row == b)[None], full, scores)
    scores = jnp.where(live[None], scores * (1.0 / math.sqrt(size)), -1e30)
    top = jnp.max(scores, axis=2, keepdims=True)
    probs = jnp.exp(scores - top)
    total = jnp.sum(probs, axis=2, keepdims=True)
    probs = probs.reshape(heads * rows, slots).astype(jnp.bfloat16)
    loads["values"].wait()
    summed = jnp.zeros((heads, rows, size), jnp.float32)
    for b in range(rows):
        full = jnp.dot(probs, v_buf[b, 0], preferred_element_type=jnp.float32)
        summed = jnp.where((out_row == b)[None], full.reshape(heads, rows, size), summed)
    part_send[:, :rows, :] = summed / total
    part_send[:, rows:, :] = jnp.broadcast_to(top + jnp.log(total), (heads, rows, size))

    pl.semaphore_wait(barrier, greeted)
    sends = []
    order = list(range(n_seq - 1, 0, -1))
    part_copies = {}
    for i in order:
        copy = pltpu.make_async_remote_copy(
            src_ref=part_send.at[seq_peers[i]],
            dst_ref=part_recv.at[i],
            send_sem=ps_sem.at[i],
            recv_sem=pr_sem.at[i],
            device_id={"seq": seq_peers[i]},
            device_id_type=MESH,
        )
        copy.start()
        part_copies[i] = copy
        sends.append(copy)

    loads["weights"].wait()
    loads["residual"].wait()
    parts = [part_send[seq]]
    for i in range(1, n_seq):
        part_copies[i].wait_recv()
        parts.append(part_recv[i])
    highest = functools.reduce(jnp.maximum, [part[rows:] for part in parts])
    factors = [jnp.exp(part[rows:] - highest) for part in parts]
    joined = sum(factor * part[:rows] for factor, part in zip(factors, parts))
    attended = (joined / sum(factors)).astype(jnp.bfloat16)

    aligned = share % 128 == 0
    if not aligned:
        for first in range(0, blocks * share, 1024):
            tile = jnp.dot(
                attended, w_buf[:, first:first + 1024], preferred_element_type=jnp.float32
            )
            for block in range(1024 // share):
                contrib[first // share + block] = tile[:, block * share:(block + 1) * share]

    def contribution(i, j, first, count):
        block = seq_peers[i] * n_kvh + kvh_peers[j]
        if not aligned:
            return contrib[block]
        columns = pl.ds(pl.multiple_of(block * share + first, 128), count)
        return jnp.dot(attended, w_buf[:, columns], preferred_element_type=jnp.float32)

    order.append(0)
    low, high = pl.ds(0, cut), pl.ds(cut, share - cut)
    direct_copies = {}
    core_copies = {}
    for i in order:
        for j in reversed(range(n_kvh)):
            if i and cut:
                direct_send[i, j] = contribution(i, j, 0, cut)
                target = {"seq": seq_peers[i]}
                if j:
                    target["kvh"] = kvh_peers[j]
                copy = pltpu.make_async_remote_copy(
                    src_ref=direct_send.at[i, j],
                    dst_ref=direct_recv.at[i, j],
                    send_sem=ds_sem.at[i, j],
                    recv_sem=dr_sem.at[i, j],
                    device_id=target,
                    device_id_type=MESH,
                )
                copy.start()
                direct_copies[i, j] = copy
                sends.append(copy)
        for j in range(1, n_kvh):
            first = cut if i else 0
            if first < share:
                part = pl.ds(first, share - first)
                core_send[i, j, :, part] = contribution(i, j, first, share - first)
                copy = pltpu.make_async_remote_copy(
                    src_ref=core_send.at[i, j, :, part],
                    dst_ref=core_recv.at[i, j, :, part],
                    send_sem=cs_sem.at[i, j],
                    recv_sem=cr_sem.at[i, j],
                    device_id={"kvh": kvh_peers[j]},
                    device_id_type=MESH,
                )
                copy.start()
                core_copies[i, j] = copy
                sends.append(copy)
    seq_copies = {}
    if cut < share:
        waiting = order[:-1]
        seq_send[waiting[0], :, high] = contribution(waiting[0], 0, cut, share - cut)
        for i, after in zip(waiting, waiting[1:] + [None]):
            if after is not None:
                seq_send[after, :, high] = contribution(after, 0, cut, share - cut)
            own = seq_send[i, :, high]
            for j in range(1, n_kvh):
                core_copies[i, j].wait_recv()
                own = own + core_recv[i, j, :, high]
            seq_send[i, :, high] = own
            copy = pltpu.make_async_remote_copy(
                src_ref=seq_send.at[i, :, high],
                dst_ref=seq_recv.at[i, :, high],
                send_sem=ss_sem.at[i],
                recv_sem=sr_sem.at[i],
                device_id={"seq": seq_peers[i]},
                device_id_type=MESH,
            )
            copy.start()
            seq_copies[i] = copy
            sends.append(copy)
    result = r_buf[...] + contribution(0, 0, 0, share)
    if cut == share:
        for i in order[:-2] + [0] + order[-2:-1]:
            for j in reversed(range(n_kvh)):
                if i:
                    direct_copies[i, j].wait_recv()
                    result = result + direct_recv[i, j]
                elif j:
                    core_copies[i, j].wait_recv()
                    result = result + core_recv[i, j]
        out[...] = result
    else:
        for j in range(1, n_kvh):
            core_copies[0, j].wait_recv()
            result = result + core_recv[0, j]
        out[...] = result
        if cut:
            result = out[:, low]
            for i in order[:-1]:
                for j in range(n_kvh):
                    direct_copies[i, j].wait_recv()
                    result = result + direct_recv[i, j]
            out[:, low] = result
        result = out[:, high]
        for i in order[:-1]:
            seq_copies[i].wait_recv()
            result = result + seq_recv[i, :, high]
        out[:, high] = result
    for copy in sends:
        copy.wait_send()


def body(n_seq, n_kvh, queries, keys, values, lengths, weights, residual):
    rows, _, heads, size = queries.shape
    slots = keys.shape[2]
    features = weights.shape[3]
    share = residual.shape[1]
    cut = min(DIRECT_COLUMNS, share) if share % 128 == 0 else 0
    f32, bf16 = jnp.float32, jnp.bfloat16
    dma = pltpu.SemaphoreType.DMA
    in_hbm = pl.BlockSpec(memory_space=pltpu.HBM)
    return pl.pallas_call(
        functools.partial(kernel, n_seq, n_kvh, cut),
        out_shape=jax.ShapeDtypeStruct((rows, share), f32),
        in_specs=[in_hbm] * 6,
        out_specs=pl.BlockSpec(memory_space=pltpu.VMEM),
        scratch_shapes=[
            pltpu.SMEM((rows,), jnp.int32),
            pltpu.VMEM((rows, 1, heads, size), bf16),
            pltpu.VMEM((rows * heads, size), f32),
            pltpu.VMEM((rows, 1, slots, size), bf16),
            pltpu.VMEM((rows, 1, slots, size), bf16),
            pltpu.VMEM((size, features), bf16),
            pltpu.VMEM((rows, share), f32),
            pltpu.VMEM((heads, 2 * rows, size), f32),
            pltpu.VMEM((n_seq, 2 * rows, size), f32),
            pltpu.VMEM((n_seq, n_kvh, rows, max(cut, 128)), f32),
            pltpu.VMEM((n_seq, n_kvh, rows, max(cut, 128)), f32),
            pltpu.VMEM((n_seq, n_kvh, rows, share), f32),
            pltpu.VMEM((n_seq, n_kvh, rows, share), f32),
            pltpu.VMEM((n_seq, rows, share), f32),
            pltpu.VMEM((n_seq, rows, share), f32),
            pltpu.VMEM((n_seq * n_kvh if share % 128 else 1, rows, share), f32),
            dma((6,)),
            dma((n_seq,)),
            dma((n_seq,)),
            dma((n_seq, n_kvh)),
            dma((n_seq, n_kvh)),
            dma((n_seq, n_kvh)),
            dma((n_seq, n_kvh)),
            dma((n_seq,)),
            dma((n_seq,)),
        ],
        compiler_params=pltpu.CompilerParams(
            collective_id=0, has_side_effects=True, vmem_limit_bytes=40 * 1024 * 1024
        ),
        cost_estimate=pl.CostEstimate(
            flops=2 * rows * size * features, bytes_accessed=2 * size * features, transcendentals=0
        ),
    )(*[
        pltpu.with_memory_space_constraint(array, pltpu.HBM)
        for array in (lengths, queries, keys, values, weights, residual)
    ])


def solution(mesh):
    in_specs = (
        P("rep", "kvh", None, None),
        P("rep", "kvh", "seq", None),
        P("rep", "kvh", "seq", None),
        P("rep"),
        P("kvh", "seq", None, None),
        P("rep", ("seq", "kvh")),
    )
    out_specs = P("rep", ("seq", "kvh"))
    run = functools.partial(body, mesh.shape["seq"], mesh.shape["kvh"])
    return jax.shard_map(run, mesh=mesh, in_specs=in_specs, out_specs=out_specs, check_vma=False)
```

```python
import functools
import math

import jax
import jax.numpy as jnp
from jax import lax
from jax.experimental import pallas as pl
from jax.experimental.pallas import tpu as pltpu
from jax.sharding import PartitionSpec as P

BLOCK_POSITIONS = 32
DIRECT_COLUMNS = 1024
MESH = pl.DeviceIdType.MESH


def partner(me, step, count):
    result = 0
    bit = 1
    while bit < count:
        own = lax.rem(lax.div(me, bit), 2)
        result = result + bit * (1 - own if (step // bit) % 2 else own)
        bit *= 2
    return result


def kernel(
    n_seq, n_kvh, cut,
    lengths, queries, keys, values, weights, residual, out,
    l_buf, q_buf, q_rows, k_buf, v_buf, w_buf, r_buf,
    part_send, part_recv, direct_send, direct_recv, core_send, core_recv,
    seq_send, seq_recv, contrib,
    load_sem, ps_sem, pr_sem, ds_sem, dr_sem, cs_sem, cr_sem, ss_sem, sr_sem,
):
    seq = lax.axis_index("seq")
    kvh = lax.axis_index("kvh")
    rows, _, heads, size = queries.shape
    slots = keys.shape[2]
    share = out.shape[1]
    blocks = n_seq * n_kvh

    loads = {
        "keys": pltpu.make_async_copy(keys, k_buf, load_sem.at[0]),
        "queries": pltpu.make_async_copy(queries, q_buf, load_sem.at[1]),
        "lengths": pltpu.make_async_copy(lengths, l_buf, load_sem.at[2]),
        "values": pltpu.make_async_copy(values, v_buf, load_sem.at[3]),
        "weights": pltpu.make_async_copy(weights.at[0, 0], w_buf, load_sem.at[4]),
        "residual": pltpu.make_async_copy(residual, r_buf, load_sem.at[5]),
    }
    for name in ("keys", "queries", "lengths", "values"):
        loads[name].start()

    seq_peers = [partner(seq, i, n_seq) for i in range(n_seq)]
    kvh_peers = [partner(kvh, j, n_kvh) for j in range(n_kvh)]
    barrier = pltpu.get_barrier_semaphore()
    greeted = 0
    for i in range(n_seq):
        for j in range(n_kvh):
            if (i or j) and (cut or not (i and j)):
                target = {"seq": seq_peers[i], "kvh": kvh_peers[j]}
                pl.semaphore_signal(barrier, inc=1, device_id=target, device_id_type=MESH)
                greeted += 1

    row = lax.broadcasted_iota(jnp.int32, (rows, slots), 0)
    slot = lax.broadcasted_iota(jnp.int32, (rows, slots), 1)
    length = jnp.zeros((rows, slots), jnp.int32)
    loads["lengths"].wait()
    for b in range(rows):
        length = jnp.where(row == b, l_buf[b], length)
    position = (slot // BLOCK_POSITIONS * n_seq + seq) * BLOCK_POSITIONS + slot % BLOCK_POSITIONS
    live = position < length
    out_row = lax.broadcasted_iota(jnp.int32, (rows, size), 0)

    loads["queries"].wait()
    for b in range(rows):
        q_rows[pl.ds(b * heads, heads), :] = q_buf[b, 0].astype(jnp.float32)
    q = jnp.concatenate(
        [q_rows[pl.ds(g, rows, stride=heads), :] for g in range(heads)], axis=0
    ).astype(jnp.bfloat16)

    loads["keys"].wait()
    loads["weights"].start()
    loads["residual"].start()
    scores = jnp.zeros((heads, rows, slots), jnp.float32)
    for b in range(rows):
        full = lax.dot_general(
            q, k_buf[b, 0], (((1,), (1,)), ((), ())), preferred_element_type=jnp.float32
        ).reshape(heads, rows, slots)
        scores = jnp.where((row == b)[None], full, scores)
    scores = jnp.where(live[None], scores * (1.0 / math.sqrt(size)), -1e30)
    top = jnp.max(scores, axis=2, keepdims=True)
    probs = jnp.exp(scores - top)
    total = jnp.sum(probs, axis=2, keepdims=True)
    probs = probs.reshape(heads * rows, slots).astype(jnp.bfloat16)
    loads["values"].wait()
    summed = jnp.zeros((heads, rows, size), jnp.float32)
    for b in range(rows):
        full = jnp.dot(probs, v_buf[b, 0], preferred_element_type=jnp.float32)
        summed = jnp.where((out_row == b)[None], full.reshape(heads, rows, size), summed)
    part_send[:, :rows, :] = summed / total
    part_send[:, rows:, :] = jnp.broadcast_to(top + jnp.log(total), (heads, rows, size))

    pl.semaphore_wait(barrier, greeted)
    sends = []
    order = list(range(n_seq - 1, 0, -1))
    part_copies = {}
    for i in order:
        copy = pltpu.make_async_remote_copy(
            src_ref=part_send.at[seq_peers[i]],
            dst_ref=part_recv.at[i],
            send_sem=ps_sem.at[i],
            recv_sem=pr_sem.at[i],
            device_id={"seq": seq_peers[i]},
            device_id_type=MESH,
        )
        copy.start()
        part_copies[i] = copy
        sends.append(copy)

    loads["weights"].wait()
    loads["residual"].wait()
    parts = [part_send[seq]]
    for i in range(1, n_seq):
        part_copies[i].wait_recv()
        parts.append(part_recv[i])
    highest = functools.reduce(jnp.maximum, [part[rows:] for part in parts])
    factors = [jnp.exp(part[rows:] - highest) for part in parts]
    joined = sum(factor * part[:rows] for factor, part in zip(factors, parts))
    attended = (joined / sum(factors)).astype(jnp.bfloat16)

    aligned = share % 128 == 0
    if not aligned:
        for first in range(0, blocks * share, 1024):
            tile = jnp.dot(
                attended, w_buf[:, first:first + 1024], preferred_element_type=jnp.float32
            )
            for block in range(1024 // share):
                contrib[first // share + block] = tile[:, block * share:(block + 1) * share]

    def contribution(i, j, first, count):
        block = seq_peers[i] * n_kvh + kvh_peers[j]
        if not aligned:
            return contrib[block]
        columns = pl.ds(pl.multiple_of(block * share + first, 128), count)
        return jnp.dot(attended, w_buf[:, columns], preferred_element_type=jnp.float32)

    order.append(0)
    low, high = pl.ds(0, cut), pl.ds(cut, share - cut)
    direct_copies = {}
    core_copies = {}
    for i in order:
        for j in range(n_kvh):
            if i and cut:
                direct_send[i, j] = contribution(i, j, 0, cut)
                target = {"seq": seq_peers[i]}
                if j:
                    target["kvh"] = kvh_peers[j]
                copy = pltpu.make_async_remote_copy(
                    src_ref=direct_send.at[i, j],
                    dst_ref=direct_recv.at[i, j],
                    send_sem=ds_sem.at[i, j],
                    recv_sem=dr_sem.at[i, j],
                    device_id=target,
                    device_id_type=MESH,
                )
                copy.start()
                direct_copies[i, j] = copy
                sends.append(copy)
        for j in range(1, n_kvh):
            first = cut if i else 0
            if first < share:
                part = pl.ds(first, share - first)
                core_send[i, j, :, part] = contribution(i, j, first, share - first)
                copy = pltpu.make_async_remote_copy(
                    src_ref=core_send.at[i, j, :, part],
                    dst_ref=core_recv.at[i, j, :, part],
                    send_sem=cs_sem.at[i, j],
                    recv_sem=cr_sem.at[i, j],
                    device_id={"kvh": kvh_peers[j]},
                    device_id_type=MESH,
                )
                copy.start()
                core_copies[i, j] = copy
                sends.append(copy)
    seq_copies = {}
    if cut < share:
        waiting = order[:-1]
        seq_send[waiting[0], :, high] = contribution(waiting[0], 0, cut, share - cut)
        for i, after in zip(waiting, waiting[1:] + [None]):
            if after is not None:
                seq_send[after, :, high] = contribution(after, 0, cut, share - cut)
            own = seq_send[i, :, high]
            for j in range(1, n_kvh):
                core_copies[i, j].wait_recv()
                own = own + core_recv[i, j, :, high]
            seq_send[i, :, high] = own
            copy = pltpu.make_async_remote_copy(
                src_ref=seq_send.at[i, :, high],
                dst_ref=seq_recv.at[i, :, high],
                send_sem=ss_sem.at[i],
                recv_sem=sr_sem.at[i],
                device_id={"seq": seq_peers[i]},
                device_id_type=MESH,
            )
            copy.start()
            seq_copies[i] = copy
            sends.append(copy)
    result = r_buf[...] + contribution(0, 0, 0, share)
    if cut == share:
        for i in order[:-2] + [0] + order[-2:-1]:
            for j in range(n_kvh):
                if i:
                    direct_copies[i, j].wait_recv()
                    result = result + direct_recv[i, j]
                elif j:
                    core_copies[i, j].wait_recv()
                    result = result + core_recv[i, j]
        out[...] = result
    else:
        for j in range(1, n_kvh):
            core_copies[0, j].wait_recv()
            result = result + core_recv[0, j]
        out[...] = result
        if cut:
            result = out[:, low]
            for i in order[:-1]:
                for j in range(n_kvh):
                    direct_copies[i, j].wait_recv()
                    result = result + direct_recv[i, j]
            out[:, low] = result
        result = out[:, high]
        for i in order[:-1]:
            seq_copies[i].wait_recv()
            result = result + seq_recv[i, :, high]
        out[:, high] = result
    for copy in sends:
        copy.wait_send()


def body(n_seq, n_kvh, queries, keys, values, lengths, weights, residual):
    rows, _, heads, size = queries.shape
    slots = keys.shape[2]
    features = weights.shape[3]
    share = residual.shape[1]
    cut = min(DIRECT_COLUMNS, share) if share % 128 == 0 else 0
    f32, bf16 = jnp.float32, jnp.bfloat16
    dma = pltpu.SemaphoreType.DMA
    in_hbm = pl.BlockSpec(memory_space=pltpu.HBM)
    return pl.pallas_call(
        functools.partial(kernel, n_seq, n_kvh, cut),
        out_shape=jax.ShapeDtypeStruct((rows, share), f32),
        in_specs=[in_hbm] * 6,
        out_specs=pl.BlockSpec(memory_space=pltpu.VMEM),
        scratch_shapes=[
            pltpu.SMEM((rows,), jnp.int32),
            pltpu.VMEM((rows, 1, heads, size), bf16),
            pltpu.VMEM((rows * heads, size), f32),
            pltpu.VMEM((rows, 1, slots, size), bf16),
            pltpu.VMEM((rows, 1, slots, size), bf16),
            pltpu.VMEM((size, features), bf16),
            pltpu.VMEM((rows, share), f32),
            pltpu.VMEM((heads, 2 * rows, size), f32),
            pltpu.VMEM((n_seq, 2 * rows, size), f32),
            pltpu.VMEM((n_seq, n_kvh, rows, max(cut, 128)), f32),
            pltpu.VMEM((n_seq, n_kvh, rows, max(cut, 128)), f32),
            pltpu.VMEM((n_seq, n_kvh, rows, share), f32),
            pltpu.VMEM((n_seq, n_kvh, rows, share), f32),
            pltpu.VMEM((n_seq, rows, share), f32),
            pltpu.VMEM((n_seq, rows, share), f32),
            pltpu.VMEM((n_seq * n_kvh if share % 128 else 1, rows, share), f32),
            dma((6,)),
            dma((n_seq,)),
            dma((n_seq,)),
            dma((n_seq, n_kvh)),
            dma((n_seq, n_kvh)),
            dma((n_seq, n_kvh)),
            dma((n_seq, n_kvh)),
            dma((n_seq,)),
            dma((n_seq,)),
        ],
        compiler_params=pltpu.CompilerParams(
            collective_id=0, has_side_effects=True, vmem_limit_bytes=40 * 1024 * 1024
        ),
        cost_estimate=pl.CostEstimate(
            flops=2 * rows * size * features, bytes_accessed=2 * size * features, transcendentals=0
        ),
    )(*[
        pltpu.with_memory_space_constraint(array, pltpu.HBM)
        for array in (lengths, queries, keys, values, weights, residual)
    ])


def solution(mesh):
    in_specs = (
        P("rep", "kvh", None, None),
        P("rep", "kvh", "seq", None),
        P("rep", "kvh", "seq", None),
        P("rep"),
        P("kvh", "seq", None, None),
        P("rep", ("seq", "kvh")),
    )
    out_specs = P("rep", ("seq", "kvh"))
    run = functools.partial(body, mesh.shape["seq"], mesh.shape["kvh"])
    return jax.shard_map(run, mesh=mesh, in_specs=in_specs, out_specs=out_specs, check_vma=False)
```

```python
import functools
import math

import jax
import jax.numpy as jnp
from jax import lax
from jax.experimental import pallas as pl
from jax.experimental.pallas import tpu as pltpu
from jax.sharding import PartitionSpec as P

BLOCK_POSITIONS = 32
DIRECT_COLUMNS = 1024
MESH = pl.DeviceIdType.MESH


def partner(me, step, count):
    result = 0
    bit = 1
    while bit < count:
        own = lax.rem(lax.div(me, bit), 2)
        result = result + bit * (1 - own if (step // bit) % 2 else own)
        bit *= 2
    return result


def kernel(
    n_seq, n_kvh, cut,
    lengths, queries, keys, values, weights, residual, out,
    l_buf, q_buf, q_rows, k_buf, v_buf, w_buf, r_buf,
    part_send, part_recv, direct_send, direct_recv, core_send, core_recv,
    seq_send, seq_recv, contrib,
    load_sem, ps_sem, pr_sem, ds_sem, dr_sem, cs_sem, cr_sem, ss_sem, sr_sem,
):
    seq = lax.axis_index("seq")
    kvh = lax.axis_index("kvh")
    rows, _, heads, size = queries.shape
    slots = keys.shape[2]
    share = out.shape[1]
    blocks = n_seq * n_kvh

    loads = {
        "keys": pltpu.make_async_copy(keys, k_buf, load_sem.at[0]),
        "queries": pltpu.make_async_copy(queries, q_buf, load_sem.at[1]),
        "lengths": pltpu.make_async_copy(lengths, l_buf, load_sem.at[2]),
        "values": pltpu.make_async_copy(values, v_buf, load_sem.at[3]),
        "weights": pltpu.make_async_copy(weights.at[0, 0], w_buf, load_sem.at[4]),
        "residual": pltpu.make_async_copy(residual, r_buf, load_sem.at[5]),
    }
    for name in ("keys", "queries", "lengths", "values"):
        loads[name].start()

    seq_peers = [partner(seq, i, n_seq) for i in range(n_seq)]
    kvh_peers = [partner(kvh, j, n_kvh) for j in range(n_kvh)]
    barrier = pltpu.get_barrier_semaphore()
    greeted = 0
    for i in range(n_seq):
        for j in range(n_kvh):
            if (i or j) and (cut or not (i and j)):
                target = {"seq": seq_peers[i], "kvh": kvh_peers[j]}
                pl.semaphore_signal(barrier, inc=1, device_id=target, device_id_type=MESH)
                greeted += 1

    row = lax.broadcasted_iota(jnp.int32, (rows, slots), 0)
    slot = lax.broadcasted_iota(jnp.int32, (rows, slots), 1)
    length = jnp.zeros((rows, slots), jnp.int32)
    loads["lengths"].wait()
    for b in range(rows):
        length = jnp.where(row == b, l_buf[b], length)
    position = (slot // BLOCK_POSITIONS * n_seq + seq) * BLOCK_POSITIONS + slot % BLOCK_POSITIONS
    live = position < length
    out_row = lax.broadcasted_iota(jnp.int32, (rows, size), 0)

    loads["queries"].wait()
    for b in range(rows):
        q_rows[pl.ds(b * heads, heads), :] = q_buf[b, 0].astype(jnp.float32)
    q = jnp.concatenate(
        [q_rows[pl.ds(g, rows, stride=heads), :] for g in range(heads)], axis=0
    ).astype(jnp.bfloat16)

    loads["keys"].wait()
    loads["weights"].start()
    loads["residual"].start()
    scores = jnp.zeros((heads, rows, slots), jnp.float32)
    for b in range(rows):
        full = lax.dot_general(
            q, k_buf[b, 0], (((1,), (1,)), ((), ())), preferred_element_type=jnp.float32
        ).reshape(heads, rows, slots)
        scores = jnp.where((row == b)[None], full, scores)
    scores = jnp.where(live[None], scores * (1.0 / math.sqrt(size)), -1e30)
    top = jnp.max(scores, axis=2, keepdims=True)
    probs = jnp.exp(scores - top)
    total = jnp.sum(probs, axis=2, keepdims=True)
    probs = probs.reshape(heads * rows, slots).astype(jnp.bfloat16)
    loads["values"].wait()
    summed = jnp.zeros((heads, rows, size), jnp.float32)
    for b in range(rows):
        full = jnp.dot(probs, v_buf[b, 0], preferred_element_type=jnp.float32)
        summed = jnp.where((out_row == b)[None], full.reshape(heads, rows, size), summed)
    part_send[:, :rows, :] = summed / total
    part_send[:, rows:, :] = jnp.broadcast_to(top + jnp.log(total), (heads, rows, size))

    pl.semaphore_wait(barrier, greeted)
    sends = []
    order = list(range(n_seq - 1, 0, -1))
    part_copies = {}
    for i in order:
        copy = pltpu.make_async_remote_copy(
            src_ref=part_send.at[seq_peers[i]],
            dst_ref=part_recv.at[i],
            send_sem=ps_sem.at[i],
            recv_sem=pr_sem.at[i],
            device_id={"seq": seq_peers[i]},
            device_id_type=MESH,
        )
        copy.start()
        part_copies[i] = copy
        sends.append(copy)

    loads["weights"].wait()
    loads["residual"].wait()
    parts = [part_send[seq]]
    for i in range(1, n_seq):
        part_copies[i].wait_recv()
        parts.append(part_recv[i])
    highest = functools.reduce(jnp.maximum, [part[rows:] for part in parts])
    factors = [jnp.exp(part[rows:] - highest) for part in parts]
    joined = sum(factor * part[:rows] for factor, part in zip(factors, parts))
    attended = (joined / sum(factors)).astype(jnp.bfloat16)

    aligned = share % 128 == 0
    if not aligned:
        for first in range(0, blocks * share, 1024):
            tile = jnp.dot(
                attended, w_buf[:, first:first + 1024], preferred_element_type=jnp.float32
            )
            for block in range(1024 // share):
                contrib[first // share + block] = tile[:, block * share:(block + 1) * share]

    def contribution(i, j, first, count):
        block = seq_peers[i] * n_kvh + kvh_peers[j]
        if not aligned:
            return contrib[block]
        columns = pl.ds(pl.multiple_of(block * share + first, 128), count)
        return jnp.dot(attended, w_buf[:, columns], preferred_element_type=jnp.float32)

    order.append(0)
    low, high = pl.ds(0, cut), pl.ds(cut, share - cut)
    direct_copies = {}
    core_copies = {}
    if cut:
        for j in range(n_kvh):
            for i in order[:-1]:
                direct_send[i, j] = contribution(i, j, 0, cut)
                target = {"seq": seq_peers[i]}
                if j:
                    target["kvh"] = kvh_peers[j]
                copy = pltpu.make_async_remote_copy(
                    src_ref=direct_send.at[i, j],
                    dst_ref=direct_recv.at[i, j],
                    send_sem=ds_sem.at[i, j],
                    recv_sem=dr_sem.at[i, j],
                    device_id=target,
                    device_id_type=MESH,
                )
                copy.start()
                direct_copies[i, j] = copy
                sends.append(copy)
    for i in order:
        for j in range(1, n_kvh):
            first = cut if i else 0
            if first < share:
                part = pl.ds(first, share - first)
                core_send[i, j, :, part] = contribution(i, j, first, share - first)
                copy = pltpu.make_async_remote_copy(
                    src_ref=core_send.at[i, j, :, part],
                    dst_ref=core_recv.at[i, j, :, part],
                    send_sem=cs_sem.at[i, j],
                    recv_sem=cr_sem.at[i, j],
                    device_id={"kvh": kvh_peers[j]},
                    device_id_type=MESH,
                )
                copy.start()
                core_copies[i, j] = copy
                sends.append(copy)
    seq_copies = {}
    if cut < share:
        waiting = order[:-1]
        seq_send[waiting[0], :, high] = contribution(waiting[0], 0, cut, share - cut)
        for i, after in zip(waiting, waiting[1:] + [None]):
            if after is not None:
                seq_send[after, :, high] = contribution(after, 0, cut, share - cut)
            own = seq_send[i, :, high]
            for j in range(1, n_kvh):
                core_copies[i, j].wait_recv()
                own = own + core_recv[i, j, :, high]
            seq_send[i, :, high] = own
            copy = pltpu.make_async_remote_copy(
                src_ref=seq_send.at[i, :, high],
                dst_ref=seq_recv.at[i, :, high],
                send_sem=ss_sem.at[i],
                recv_sem=sr_sem.at[i],
                device_id={"seq": seq_peers[i]},
                device_id_type=MESH,
            )
            copy.start()
            seq_copies[i] = copy
            sends.append(copy)
    result = r_buf[...] + contribution(0, 0, 0, share)
    if cut == share:
        for j in range(n_kvh):
            for i in order[:-1]:
                direct_copies[i, j].wait_recv()
                result = result + direct_recv[i, j]
        for j in range(1, n_kvh):
            core_copies[0, j].wait_recv()
            result = result + core_recv[0, j]
        out[...] = result
    else:
        for j in range(1, n_kvh):
            core_copies[0, j].wait_recv()
            result = result + core_recv[0, j]
        out[...] = result
        if cut:
            result = out[:, low]
            for i in order[:-1]:
                for j in range(n_kvh):
                    direct_copies[i, j].wait_recv()
                    result = result + direct_recv[i, j]
            out[:, low] = result
        result = out[:, high]
        for i in order[:-1]:
            seq_copies[i].wait_recv()
            result = result + seq_recv[i, :, high]
        out[:, high] = result
    for copy in sends:
        copy.wait_send()


def body(n_seq, n_kvh, queries, keys, values, lengths, weights, residual):
    rows, _, heads, size = queries.shape
    slots = keys.shape[2]
    features = weights.shape[3]
    share = residual.shape[1]
    cut = min(DIRECT_COLUMNS, share) if share % 128 == 0 else 0
    f32, bf16 = jnp.float32, jnp.bfloat16
    dma = pltpu.SemaphoreType.DMA
    in_hbm = pl.BlockSpec(memory_space=pltpu.HBM)
    return pl.pallas_call(
        functools.partial(kernel, n_seq, n_kvh, cut),
        out_shape=jax.ShapeDtypeStruct((rows, share), f32),
        in_specs=[in_hbm] * 6,
        out_specs=pl.BlockSpec(memory_space=pltpu.VMEM),
        scratch_shapes=[
            pltpu.SMEM((rows,), jnp.int32),
            pltpu.VMEM((rows, 1, heads, size), bf16),
            pltpu.VMEM((rows * heads, size), f32),
            pltpu.VMEM((rows, 1, slots, size), bf16),
            pltpu.VMEM((rows, 1, slots, size), bf16),
            pltpu.VMEM((size, features), bf16),
            pltpu.VMEM((rows, share), f32),
            pltpu.VMEM((heads, 2 * rows, size), f32),
            pltpu.VMEM((n_seq, 2 * rows, size), f32),
            pltpu.VMEM((n_seq, n_kvh, rows, max(cut, 128)), f32),
            pltpu.VMEM((n_seq, n_kvh, rows, max(cut, 128)), f32),
            pltpu.VMEM((n_seq, n_kvh, rows, share), f32),
            pltpu.VMEM((n_seq, n_kvh, rows, share), f32),
            pltpu.VMEM((n_seq, rows, share), f32),
            pltpu.VMEM((n_seq, rows, share), f32),
            pltpu.VMEM((n_seq * n_kvh if share % 128 else 1, rows, share), f32),
            dma((6,)),
            dma((n_seq,)),
            dma((n_seq,)),
            dma((n_seq, n_kvh)),
            dma((n_seq, n_kvh)),
            dma((n_seq, n_kvh)),
            dma((n_seq, n_kvh)),
            dma((n_seq,)),
            dma((n_seq,)),
        ],
        compiler_params=pltpu.CompilerParams(
            collective_id=0, has_side_effects=True, vmem_limit_bytes=40 * 1024 * 1024
        ),
        cost_estimate=pl.CostEstimate(
            flops=2 * rows * size * features, bytes_accessed=2 * size * features, transcendentals=0
        ),
    )(*[
        pltpu.with_memory_space_constraint(array, pltpu.HBM)
        for array in (lengths, queries, keys, values, weights, residual)
    ])


def solution(mesh):
    in_specs = (
        P("rep", "kvh", None, None),
        P("rep", "kvh", "seq", None),
        P("rep", "kvh", "seq", None),
        P("rep"),
        P("kvh", "seq", None, None),
        P("rep", ("seq", "kvh")),
    )
    out_specs = P("rep", ("seq", "kvh"))
    run = functools.partial(body, mesh.shape["seq"], mesh.shape["kvh"])
    return jax.shard_map(run, mesh=mesh, in_specs=in_specs, out_specs=out_specs, check_vma=False)
```

```python
import functools
import math

import jax
import jax.numpy as jnp
from jax import lax
from jax.experimental import pallas as pl
from jax.experimental.pallas import tpu as pltpu
from jax.sharding import PartitionSpec as P

BLOCK_POSITIONS = 32
DIRECT_COLUMNS = 1024
MESH = pl.DeviceIdType.MESH


def partner(me, step, count):
    result = 0
    bit = 1
    while bit < count:
        own = lax.rem(lax.div(me, bit), 2)
        result = result + bit * (1 - own if (step // bit) % 2 else own)
        bit *= 2
    return result


def kernel(
    n_seq, n_kvh, cut,
    lengths, queries, keys, values, weights, residual, out,
    l_buf, q_buf, q_rows, k_buf, v_buf, w_buf, r_buf,
    part_send, part_recv, direct_send, direct_recv, core_send, core_recv,
    seq_send, seq_recv, contrib,
    load_sem, ps_sem, pr_sem, ds_sem, dr_sem, cs_sem, cr_sem, ss_sem, sr_sem,
):
    seq = lax.axis_index("seq")
    kvh = lax.axis_index("kvh")
    rows, _, heads, size = queries.shape
    slots = keys.shape[2]
    share = out.shape[1]
    blocks = n_seq * n_kvh

    pieces = 4 if rows % 4 == 0 else 1
    step = rows // pieces
    loads = {}
    for n in range(pieces):
        some = pl.ds(n * step, step)
        loads["keys", n * step] = pltpu.make_async_copy(
            keys.at[some], k_buf.at[some], load_sem.at[5 + n]
        )
        loads["keys", n * step].start()
        if n == 0:
            loads["queries"] = pltpu.make_async_copy(queries, q_buf, load_sem.at[0])
            loads["queries"].start()
    loads["lengths"] = pltpu.make_async_copy(lengths, l_buf, load_sem.at[1])
    loads["values"] = pltpu.make_async_copy(values, v_buf, load_sem.at[2])
    loads["lengths"].start()
    loads["values"].start()
    loads["weights"] = pltpu.make_async_copy(weights.at[0, 0], w_buf, load_sem.at[3])
    loads["residual"] = pltpu.make_async_copy(residual, r_buf, load_sem.at[4])

    seq_peers = [partner(seq, i, n_seq) for i in range(n_seq)]
    kvh_peers = [partner(kvh, j, n_kvh) for j in range(n_kvh)]
    barrier = pltpu.get_barrier_semaphore()
    greeted = 0
    for i in range(n_seq):
        for j in range(n_kvh):
            if (i or j) and (cut or not (i and j)):
                target = {"seq": seq_peers[i], "kvh": kvh_peers[j]}
                pl.semaphore_signal(barrier, inc=1, device_id=target, device_id_type=MESH)
                greeted += 1

    row = lax.broadcasted_iota(jnp.int32, (rows, slots), 0)
    slot = lax.broadcasted_iota(jnp.int32, (rows, slots), 1)
    length = jnp.zeros((rows, slots), jnp.int32)
    loads["lengths"].wait()
    for b in range(rows):
        length = jnp.where(row == b, l_buf[b], length)
    position = (slot // BLOCK_POSITIONS * n_seq + seq) * BLOCK_POSITIONS + slot % BLOCK_POSITIONS
    live = position < length
    out_row = lax.broadcasted_iota(jnp.int32, (rows, size), 0)

    loads["queries"].wait()
    for b in range(rows):
        q_rows[pl.ds(b * heads, heads), :] = q_buf[b, 0].astype(jnp.float32)
    q = jnp.concatenate(
        [q_rows[pl.ds(g, rows, stride=heads), :] for g in range(heads)], axis=0
    ).astype(jnp.bfloat16)

    scores = jnp.zeros((heads, rows, slots), jnp.float32)
    for b in range(rows):
        if b % step == 0:
            loads["keys", b].wait()
        full = lax.dot_general(
            q, k_buf[b, 0], (((1,), (1,)), ((), ())), preferred_element_type=jnp.float32
        ).reshape(heads, rows, slots)
        scores = jnp.where((row == b)[None], full, scores)
    loads["weights"].start()
    loads["residual"].start()
    scores = jnp.where(live[None], scores * (1.0 / math.sqrt(size)), -1e30)
    top = jnp.max(scores, axis=2, keepdims=True)
    probs = jnp.exp(scores - top)
    total = jnp.sum(probs, axis=2, keepdims=True)
    probs = probs.reshape(heads * rows, slots).astype(jnp.bfloat16)
    loads["values"].wait()
    summed = jnp.zeros((heads, rows, size), jnp.float32)
    for b in range(rows):
        full = jnp.dot(probs, v_buf[b, 0], preferred_element_type=jnp.float32)
        summed = jnp.where((out_row == b)[None], full.reshape(heads, rows, size), summed)
    part_send[:, :rows, :] = summed / total
    part_send[:, rows:, :] = jnp.broadcast_to(top + jnp.log(total), (heads, rows, size))

    pl.semaphore_wait(barrier, greeted)
    sends = []
    order = list(range(n_seq - 1, 0, -1))
    part_copies = {}
    for i in order:
        copy = pltpu.make_async_remote_copy(
            src_ref=part_send.at[seq_peers[i]],
            dst_ref=part_recv.at[i],
            send_sem=ps_sem.at[i],
            recv_sem=pr_sem.at[i],
            device_id={"seq": seq_peers[i]},
            device_id_type=MESH,
        )
        copy.start()
        part_copies[i] = copy
        sends.append(copy)

    loads["weights"].wait()
    loads["residual"].wait()
    parts = [part_send[seq]]
    for i in range(1, n_seq):
        part_copies[i].wait_recv()
        parts.append(part_recv[i])
    highest = functools.reduce(jnp.maximum, [part[rows:] for part in parts])
    factors = [jnp.exp(part[rows:] - highest) for part in parts]
    joined = sum(factor * part[:rows] for factor, part in zip(factors, parts))
    attended = (joined / sum(factors)).astype(jnp.bfloat16)

    aligned = share % 128 == 0
    if not aligned:
        for first in range(0, blocks * share, 1024):
            tile = jnp.dot(
                attended, w_buf[:, first:first + 1024], preferred_element_type=jnp.float32
            )
            for block in range(1024 // share):
                contrib[first // share + block] = tile[:, block * share:(block + 1) * share]

    def contribution(i, j, first, count):
        block = seq_peers[i] * n_kvh + kvh_peers[j]
        if not aligned:
            return contrib[block]
        columns = pl.ds(pl.multiple_of(block * share + first, 128), count)
        return jnp.dot(attended, w_buf[:, columns], preferred_element_type=jnp.float32)

    order.append(0)
    low, high = pl.ds(0, cut), pl.ds(cut, share - cut)
    direct_copies = {}
    core_copies = {}
    if cut:
        for j in range(n_kvh):
            for i in order[:-1]:
                direct_send[i, j] = contribution(i, j, 0, cut)
                target = {"seq": seq_peers[i]}
                if j:
                    target["kvh"] = kvh_peers[j]
                copy = pltpu.make_async_remote_copy(
                    src_ref=direct_send.at[i, j],
                    dst_ref=direct_recv.at[i, j],
                    send_sem=ds_sem.at[i, j],
                    recv_sem=dr_sem.at[i, j],
                    device_id=target,
                    device_id_type=MESH,
                )
                copy.start()
                direct_copies[i, j] = copy
                sends.append(copy)
    for i in order:
        for j in range(1, n_kvh):
            first = cut if i else 0
            if first < share:
                part = pl.ds(first, share - first)
                core_send[i, j, :, part] = contribution(i, j, first, share - first)
                copy = pltpu.make_async_remote_copy(
                    src_ref=core_send.at[i, j, :, part],
                    dst_ref=core_recv.at[i, j, :, part],
                    send_sem=cs_sem.at[i, j],
                    recv_sem=cr_sem.at[i, j],
                    device_id={"kvh": kvh_peers[j]},
                    device_id_type=MESH,
                )
                copy.start()
                core_copies[i, j] = copy
                sends.append(copy)
    seq_copies = {}
    if cut < share:
        waiting = order[:-1]
        seq_send[waiting[0], :, high] = contribution(waiting[0], 0, cut, share - cut)
        for i, after in zip(waiting, waiting[1:] + [None]):
            if after is not None:
                seq_send[after, :, high] = contribution(after, 0, cut, share - cut)
            own = seq_send[i, :, high]
            for j in range(1, n_kvh):
                core_copies[i, j].wait_recv()
                own = own + core_recv[i, j, :, high]
            seq_send[i, :, high] = own
            copy = pltpu.make_async_remote_copy(
                src_ref=seq_send.at[i, :, high],
                dst_ref=seq_recv.at[i, :, high],
                send_sem=ss_sem.at[i],
                recv_sem=sr_sem.at[i],
                device_id={"seq": seq_peers[i]},
                device_id_type=MESH,
            )
            copy.start()
            seq_copies[i] = copy
            sends.append(copy)
    result = r_buf[...] + contribution(0, 0, 0, share)
    if cut == share:
        for j in range(n_kvh):
            for i in order[:-1]:
                direct_copies[i, j].wait_recv()
                result = result + direct_recv[i, j]
        for j in range(1, n_kvh):
            core_copies[0, j].wait_recv()
            result = result + core_recv[0, j]
        out[...] = result
    else:
        for j in range(1, n_kvh):
            core_copies[0, j].wait_recv()
            result = result + core_recv[0, j]
        out[...] = result
        if cut:
            result = out[:, low]
            for i in order[:-1]:
                for j in range(n_kvh):
                    direct_copies[i, j].wait_recv()
                    result = result + direct_recv[i, j]
            out[:, low] = result
        result = out[:, high]
        for i in order[:-1]:
            seq_copies[i].wait_recv()
            result = result + seq_recv[i, :, high]
        out[:, high] = result
    for copy in sends:
        copy.wait_send()


def body(n_seq, n_kvh, queries, keys, values, lengths, weights, residual):
    rows, _, heads, size = queries.shape
    slots = keys.shape[2]
    features = weights.shape[3]
    share = residual.shape[1]
    cut = min(DIRECT_COLUMNS, share) if share % 128 == 0 else 0
    f32, bf16 = jnp.float32, jnp.bfloat16
    dma = pltpu.SemaphoreType.DMA
    in_hbm = pl.BlockSpec(memory_space=pltpu.HBM)
    return pl.pallas_call(
        functools.partial(kernel, n_seq, n_kvh, cut),
        out_shape=jax.ShapeDtypeStruct((rows, share), f32),
        in_specs=[in_hbm] * 6,
        out_specs=pl.BlockSpec(memory_space=pltpu.VMEM),
        scratch_shapes=[
            pltpu.SMEM((rows,), jnp.int32),
            pltpu.VMEM((rows, 1, heads, size), bf16),
            pltpu.VMEM((rows * heads, size), f32),
            pltpu.VMEM((rows, 1, slots, size), bf16),
            pltpu.VMEM((rows, 1, slots, size), bf16),
            pltpu.VMEM((size, features), bf16),
            pltpu.VMEM((rows, share), f32),
            pltpu.VMEM((heads, 2 * rows, size), f32),
            pltpu.VMEM((n_seq, 2 * rows, size), f32),
            pltpu.VMEM((n_seq, n_kvh, rows, max(cut, 128)), f32),
            pltpu.VMEM((n_seq, n_kvh, rows, max(cut, 128)), f32),
            pltpu.VMEM((n_seq, n_kvh, rows, share), f32),
            pltpu.VMEM((n_seq, n_kvh, rows, share), f32),
            pltpu.VMEM((n_seq, rows, share), f32),
            pltpu.VMEM((n_seq, rows, share), f32),
            pltpu.VMEM((n_seq * n_kvh if share % 128 else 1, rows, share), f32),
            dma((9,)),
            dma((n_seq,)),
            dma((n_seq,)),
            dma((n_seq, n_kvh)),
            dma((n_seq, n_kvh)),
            dma((n_seq, n_kvh)),
            dma((n_seq, n_kvh)),
            dma((n_seq,)),
            dma((n_seq,)),
        ],
        compiler_params=pltpu.CompilerParams(
            collective_id=0, has_side_effects=True, vmem_limit_bytes=40 * 1024 * 1024
        ),
        cost_estimate=pl.CostEstimate(
            flops=2 * rows * size * features, bytes_accessed=2 * size * features, transcendentals=0
        ),
    )(*[
        pltpu.with_memory_space_constraint(array, pltpu.HBM)
        for array in (lengths, queries, keys, values, weights, residual)
    ])


def solution(mesh):
    in_specs = (
        P("rep", "kvh", None, None),
        P("rep", "kvh", "seq", None),
        P("rep", "kvh", "seq", None),
        P("rep"),
        P("kvh", "seq", None, None),
        P("rep", ("seq", "kvh")),
    )
    out_specs = P("rep", ("seq", "kvh"))
    run = functools.partial(body, mesh.shape["seq"], mesh.shape["kvh"])
    return jax.shard_map(run, mesh=mesh, in_specs=in_specs, out_specs=out_specs, check_vma=False)
```

```python
import functools
import math

import jax
import jax.numpy as jnp
from jax import lax
from jax.experimental import pallas as pl
from jax.experimental.pallas import tpu as pltpu
from jax.sharding import PartitionSpec as P

BLOCK_POSITIONS = 32
MESH = pl.DeviceIdType.MESH


def partner(me, step, count):
    result = 0
    bit = 1
    while bit < count:
        own = lax.rem(lax.div(me, bit), 2)
        result = result + bit * (1 - own if (step // bit) % 2 else own)
        bit *= 2
    return result


def kernel(
    n_seq, n_kvh,
    lengths, queries, keys, values, weights, residual, out,
    l_buf, q_buf, q_rows, k_buf, v_buf, w_buf, r_buf,
    part_send, part_recv, direct_send, direct_recv, contrib,
    load_sem, ps_sem, pr_sem, ds_sem, dr_sem,
):
    seq = lax.axis_index("seq")
    kvh = lax.axis_index("kvh")
    rows, _, heads, size = queries.shape
    slots = keys.shape[2]
    share = out.shape[1]
    blocks = n_seq * n_kvh

    loads = {
        "keys": pltpu.make_async_copy(keys, k_buf, load_sem.at[0]),
        "queries": pltpu.make_async_copy(queries, q_buf, load_sem.at[1]),
        "lengths": pltpu.make_async_copy(lengths, l_buf, load_sem.at[2]),
        "values": pltpu.make_async_copy(values, v_buf, load_sem.at[3]),
        "weights": pltpu.make_async_copy(weights.at[0, 0], w_buf, load_sem.at[4]),
        "residual": pltpu.make_async_copy(residual, r_buf, load_sem.at[5]),
    }
    for name in ("keys", "queries", "lengths", "values"):
        loads[name].start()

    seq_peers = [partner(seq, i, n_seq) for i in range(n_seq)]
    kvh_peers = [partner(kvh, j, n_kvh) for j in range(n_kvh)]
    barrier = pltpu.get_barrier_semaphore()
    greeted = 0
    for i in range(n_seq):
        for j in range(n_kvh):
            if i or j:
                target = {"seq": seq_peers[i], "kvh": kvh_peers[j]}
                pl.semaphore_signal(barrier, inc=1, device_id=target, device_id_type=MESH)
                greeted += 1

    row = lax.broadcasted_iota(jnp.int32, (rows, slots), 0)
    slot = lax.broadcasted_iota(jnp.int32, (rows, slots), 1)
    length = jnp.zeros((rows, slots), jnp.int32)
    loads["lengths"].wait()
    for b in range(rows):
        length = jnp.where(row == b, l_buf[b], length)
    position = (slot // BLOCK_POSITIONS * n_seq + seq) * BLOCK_POSITIONS + slot % BLOCK_POSITIONS
    live = position < length
    out_row = lax.broadcasted_iota(jnp.int32, (rows, size), 0)

    loads["queries"].wait()
    for b in range(rows):
        q_rows[pl.ds(b * heads, heads), :] = q_buf[b, 0].astype(jnp.float32)
    q = jnp.concatenate(
        [q_rows[pl.ds(g, rows, stride=heads), :] for g in range(heads)], axis=0
    ).astype(jnp.bfloat16)

    loads["keys"].wait()
    loads["weights"].start()
    loads["residual"].start()
    scores = jnp.zeros((heads, rows, slots), jnp.float32)
    for b in range(rows):
        full = lax.dot_general(
            q, k_buf[b, 0], (((1,), (1,)), ((), ())), preferred_element_type=jnp.float32
        ).reshape(heads, rows, slots)
        scores = jnp.where((row == b)[None], full, scores)
    scores = jnp.where(live[None], scores * (1.0 / math.sqrt(size)), -1e30)
    top = jnp.max(scores, axis=2, keepdims=True)
    probs = jnp.exp(scores - top)
    total = jnp.sum(probs, axis=2, keepdims=True)
    probs = probs.reshape(heads * rows, slots).astype(jnp.bfloat16)
    loads["values"].wait()
    summed = jnp.zeros((heads, rows, size), jnp.float32)
    for b in range(rows):
        full = jnp.dot(probs, v_buf[b, 0], preferred_element_type=jnp.float32)
        summed = jnp.where((out_row == b)[None], full.reshape(heads, rows, size), summed)
    part_send[:, :rows, :] = summed / total
    part_send[:, rows:, :] = jnp.broadcast_to(top + jnp.log(total), (heads, rows, size))

    pl.semaphore_wait(barrier, greeted)
    order = list(range(n_seq - 1, 0, -1))
    for i in order:
        pltpu.make_async_remote_copy(
            src_ref=part_send.at[seq_peers[i]],
            dst_ref=part_recv.at[i - 1],
            send_sem=ps_sem,
            recv_sem=pr_sem,
            device_id={"seq": seq_peers[i]},
            device_id_type=MESH,
        ).start()

    loads["weights"].wait()
    loads["residual"].wait()
    pltpu.make_async_copy(part_recv, part_recv, pr_sem).wait()
    parts = [part_send[seq]] + [part_recv[i] for i in range(n_seq - 1)]
    highest = functools.reduce(jnp.maximum, [part[rows:] for part in parts])
    factors = [jnp.exp(part[rows:] - highest) for part in parts]
    joined = sum(factor * part[:rows] for factor, part in zip(factors, parts))
    attended = (joined / sum(factors)).astype(jnp.bfloat16)

    aligned = share % 128 == 0
    if not aligned:
        for first in range(0, blocks * share, 1024):
            tile = jnp.dot(
                attended, w_buf[:, first:first + 1024], preferred_element_type=jnp.float32
            )
            for block in range(1024 // share):
                contrib[first // share + block] = tile[:, block * share:(block + 1) * share]

    def contribution(block):
        if not aligned:
            return contrib[block]
        columns = pl.ds(pl.multiple_of(block * share, 128), share)
        return jnp.dot(attended, w_buf[:, columns], preferred_element_type=jnp.float32)

    pairs = [(i, j) for j in range(n_kvh) for i in order] + [(0, j) for j in range(1, n_kvh)]
    for i, j in pairs:
        slot = i * n_kvh + j - 1
        direct_send[slot] = contribution(seq_peers[i] * n_kvh + kvh_peers[j])
        target = {"seq": seq_peers[i], "kvh": kvh_peers[j]}
        pltpu.make_async_remote_copy(
            src_ref=direct_send.at[slot],
            dst_ref=direct_recv.at[slot],
            send_sem=ds_sem,
            recv_sem=dr_sem,
            device_id=target,
            device_id_type=MESH,
        ).start()
    result = r_buf[...] + contribution(seq * n_kvh + kvh)
    pltpu.make_async_copy(part_recv, part_recv, ps_sem).wait()
    pltpu.make_async_copy(direct_recv, direct_recv, dr_sem).wait()
    for slot in range(blocks - 1):
        result = result + direct_recv[slot]
    out[...] = result
    pltpu.make_async_copy(direct_send, direct_send, ds_sem).wait()


def body(n_seq, n_kvh, queries, keys, values, lengths, weights, residual):
    rows, _, heads, size = queries.shape
    slots = keys.shape[2]
    features = weights.shape[3]
    share = residual.shape[1]
    f32, bf16 = jnp.float32, jnp.bfloat16
    dma = pltpu.SemaphoreType.DMA
    in_hbm = pl.BlockSpec(memory_space=pltpu.HBM)
    return pl.pallas_call(
        functools.partial(kernel, n_seq, n_kvh),
        out_shape=jax.ShapeDtypeStruct((rows, share), f32),
        in_specs=[in_hbm] * 6,
        out_specs=pl.BlockSpec(memory_space=pltpu.VMEM),
        scratch_shapes=[
            pltpu.SMEM((rows,), jnp.int32),
            pltpu.VMEM((rows, 1, heads, size), bf16),
            pltpu.VMEM((rows * heads, size), f32),
            pltpu.VMEM((rows, 1, slots, size), bf16),
            pltpu.VMEM((rows, 1, slots, size), bf16),
            pltpu.VMEM((size, features), bf16),
            pltpu.VMEM((rows, share), f32),
            pltpu.VMEM((heads, 2 * rows, size), f32),
            pltpu.VMEM((n_seq - 1, 2 * rows, size), f32),
            pltpu.VMEM((n_seq * n_kvh - 1, rows, share), f32),
            pltpu.VMEM((n_seq * n_kvh - 1, rows, share), f32),
            pltpu.VMEM((n_seq * n_kvh if share % 128 else 1, rows, share), f32),
            dma((6,)),
            dma,
            dma,
            dma,
            dma,
        ],
        compiler_params=pltpu.CompilerParams(
            collective_id=0, has_side_effects=True, vmem_limit_bytes=40 * 1024 * 1024
        ),
        cost_estimate=pl.CostEstimate(
            flops=2 * rows * size * features, bytes_accessed=2 * size * features, transcendentals=0
        ),
    )(*[
        pltpu.with_memory_space_constraint(array, pltpu.HBM)
        for array in (lengths, queries, keys, values, weights, residual)
    ])


def solution(mesh):
    in_specs = (
        P("rep", "kvh", None, None),
        P("rep", "kvh", "seq", None),
        P("rep", "kvh", "seq", None),
        P("rep"),
        P("kvh", "seq", None, None),
        P("rep", ("seq", "kvh")),
    )
    out_specs = P("rep", ("seq", "kvh"))
    run = functools.partial(body, mesh.shape["seq"], mesh.shape["kvh"])
    return jax.shard_map(run, mesh=mesh, in_specs=in_specs, out_specs=out_specs, check_vma=False)
```

```python
import functools
import math

import jax
import jax.numpy as jnp
from jax import lax
from jax.experimental import pallas as pl
from jax.experimental.pallas import tpu as pltpu
from jax.sharding import PartitionSpec as P

BLOCK_POSITIONS = 32
MESH = pl.DeviceIdType.MESH


def partner(me, step, count):
    result = 0
    bit = 1
    while bit < count:
        own = lax.rem(lax.div(me, bit), 2)
        result = result + bit * (1 - own if (step // bit) % 2 else own)
        bit *= 2
    return result


def kernel(
    n_seq, n_kvh,
    lengths, queries, keys, values, weights, residual, out,
    l_buf, q_buf, q_rows, k_buf, v_buf, w_buf, r_buf,
    part_send, part_recv, direct_send, direct_recv, contrib,
    load_sem, ps_sem, pr_sem, ds_sem, dr_sem,
):
    seq = lax.axis_index("seq")
    kvh = lax.axis_index("kvh")
    rows, _, heads, size = queries.shape
    slots = keys.shape[2]
    share = out.shape[1]
    blocks = n_seq * n_kvh

    loads = {
        "keys": pltpu.make_async_copy(keys, k_buf, load_sem.at[0]),
        "queries": pltpu.make_async_copy(queries, q_buf, load_sem.at[1]),
        "lengths": pltpu.make_async_copy(lengths, l_buf, load_sem.at[2]),
        "values": pltpu.make_async_copy(values, v_buf, load_sem.at[3]),
        "weights": pltpu.make_async_copy(weights.at[0, 0], w_buf, load_sem.at[4]),
        "residual": pltpu.make_async_copy(residual, r_buf, load_sem.at[5]),
    }
    for name in ("keys", "queries", "lengths", "values"):
        loads[name].start()

    seq_peers = [partner(seq, i, n_seq) for i in range(n_seq)]
    kvh_peers = [partner(kvh, j, n_kvh) for j in range(n_kvh)]
    barrier = pltpu.get_barrier_semaphore()
    greeted = 0
    for i in range(n_seq):
        for j in range(n_kvh):
            if i or j:
                target = {"seq": seq_peers[i], "kvh": kvh_peers[j]}
                pl.semaphore_signal(barrier, inc=1, device_id=target, device_id_type=MESH)
                greeted += 1

    row = lax.broadcasted_iota(jnp.int32, (rows, slots), 0)
    slot = lax.broadcasted_iota(jnp.int32, (rows, slots), 1)
    length = jnp.zeros((rows, slots), jnp.int32)
    loads["lengths"].wait()
    for b in range(rows):
        length = jnp.where(row == b, l_buf[b], length)
    position = (slot // BLOCK_POSITIONS * n_seq + seq) * BLOCK_POSITIONS + slot % BLOCK_POSITIONS
    live = position < length
    out_row = lax.broadcasted_iota(jnp.int32, (rows, size), 0)

    loads["queries"].wait()
    for b in range(rows):
        q_rows[pl.ds(b * heads, heads), :] = q_buf[b, 0].astype(jnp.float32)
    q = jnp.concatenate(
        [q_rows[pl.ds(g, rows, stride=heads), :] for g in range(heads)], axis=0
    ).astype(jnp.bfloat16)

    loads["keys"].wait()
    loads["weights"].start()
    loads["residual"].start()
    scores = jnp.zeros((heads, rows, slots), jnp.float32)
    for b in range(rows):
        full = lax.dot_general(
            q, k_buf[b, 0], (((1,), (1,)), ((), ())), preferred_element_type=jnp.float32
        ).reshape(heads, rows, slots)
        scores = jnp.where((row == b)[None], full, scores)
    scores = jnp.where(live[None], scores * (1.0 / math.sqrt(size)), -1e30)
    top = jnp.max(scores, axis=2, keepdims=True)
    probs = jnp.exp(scores - top)
    total = jnp.sum(probs, axis=2, keepdims=True)
    probs = probs.reshape(heads * rows, slots).astype(jnp.bfloat16)
    loads["values"].wait()
    summed = jnp.zeros((heads, rows, size), jnp.float32)
    for b in range(rows):
        full = jnp.dot(probs, v_buf[b, 0], preferred_element_type=jnp.float32)
        summed = jnp.where((out_row == b)[None], full.reshape(heads, rows, size), summed)
    part_send[:, :rows, :] = summed / total
    part_send[:, rows:, :] = jnp.broadcast_to(top + jnp.log(total), (heads, rows, size))

    pl.semaphore_wait(barrier, greeted)
    order = list(range(n_seq - 1, 0, -1))
    for i in order:
        pltpu.make_async_remote_copy(
            src_ref=part_send.at[seq_peers[i]],
            dst_ref=part_recv.at[i - 1],
            send_sem=ps_sem,
            recv_sem=pr_sem,
            device_id={"seq": seq_peers[i]},
            device_id_type=MESH,
        ).start()

    loads["weights"].wait()
    loads["residual"].wait()
    pltpu.make_async_copy(part_recv, part_recv, pr_sem).wait()
    parts = [part_send[seq]] + [part_recv[i] for i in range(n_seq - 1)]
    highest = functools.reduce(jnp.maximum, [part[rows:] for part in parts])
    factors = [jnp.exp(part[rows:] - highest) for part in parts]
    joined = sum(factor * part[:rows] for factor, part in zip(factors, parts))
    attended = (joined / sum(factors)).astype(jnp.bfloat16)

    aligned = share % 128 == 0
    if not aligned:
        for first in range(0, blocks * share, 1024):
            tile = jnp.dot(
                attended, w_buf[:, first:first + 1024], preferred_element_type=jnp.float32
            )
            for block in range(1024 // share):
                contrib[first // share + block] = tile[:, block * share:(block + 1) * share]

    def contribution(block):
        if not aligned:
            return contrib[block]
        columns = pl.ds(pl.multiple_of(block * share, 128), share)
        return jnp.dot(attended, w_buf[:, columns], preferred_element_type=jnp.float32)

    pairs = [(i, j) for j in range(n_kvh) for i in order] + [(0, j) for j in range(1, n_kvh)]
    done = 0
    while done < len(pairs):
        group = pairs[done:2 * done + 1]
        done += len(group)
        for i, j in group:
            direct_send[i * n_kvh + j - 1] = contribution(seq_peers[i] * n_kvh + kvh_peers[j])
        for i, j in group:
            slot = i * n_kvh + j - 1
            pltpu.make_async_remote_copy(
                src_ref=direct_send.at[slot],
                dst_ref=direct_recv.at[slot],
                send_sem=ds_sem,
                recv_sem=dr_sem,
                device_id={"seq": seq_peers[i], "kvh": kvh_peers[j]},
                device_id_type=MESH,
            ).start()
    result = r_buf[...] + contribution(seq * n_kvh + kvh)
    pltpu.make_async_copy(part_recv, part_recv, ps_sem).wait()
    pltpu.make_async_copy(direct_recv, direct_recv, dr_sem).wait()
    for slot in range(blocks - 1):
        result = result + direct_recv[slot]
    out[...] = result
    pltpu.make_async_copy(direct_send, direct_send, ds_sem).wait()


def body(n_seq, n_kvh, queries, keys, values, lengths, weights, residual):
    rows, _, heads, size = queries.shape
    slots = keys.shape[2]
    features = weights.shape[3]
    share = residual.shape[1]
    f32, bf16 = jnp.float32, jnp.bfloat16
    dma = pltpu.SemaphoreType.DMA
    in_hbm = pl.BlockSpec(memory_space=pltpu.HBM)
    return pl.pallas_call(
        functools.partial(kernel, n_seq, n_kvh),
        out_shape=jax.ShapeDtypeStruct((rows, share), f32),
        in_specs=[in_hbm] * 6,
        out_specs=pl.BlockSpec(memory_space=pltpu.VMEM),
        scratch_shapes=[
            pltpu.SMEM((rows,), jnp.int32),
            pltpu.VMEM((rows, 1, heads, size), bf16),
            pltpu.VMEM((rows * heads, size), f32),
            pltpu.VMEM((rows, 1, slots, size), bf16),
            pltpu.VMEM((rows, 1, slots, size), bf16),
            pltpu.VMEM((size, features), bf16),
            pltpu.VMEM((rows, share), f32),
            pltpu.VMEM((heads, 2 * rows, size), f32),
            pltpu.VMEM((n_seq - 1, 2 * rows, size), f32),
            pltpu.VMEM((n_seq * n_kvh - 1, rows, share), f32),
            pltpu.VMEM((n_seq * n_kvh - 1, rows, share), f32),
            pltpu.VMEM((n_seq * n_kvh if share % 128 else 1, rows, share), f32),
            dma((6,)),
            dma,
            dma,
            dma,
            dma,
        ],
        compiler_params=pltpu.CompilerParams(
            collective_id=0, has_side_effects=True, vmem_limit_bytes=40 * 1024 * 1024
        ),
        cost_estimate=pl.CostEstimate(
            flops=2 * rows * size * features, bytes_accessed=2 * size * features, transcendentals=0
        ),
    )(*[
        pltpu.with_memory_space_constraint(array, pltpu.HBM)
        for array in (lengths, queries, keys, values, weights, residual)
    ])


def solution(mesh):
    in_specs = (
        P("rep", "kvh", None, None),
        P("rep", "kvh", "seq", None),
        P("rep", "kvh", "seq", None),
        P("rep"),
        P("kvh", "seq", None, None),
        P("rep", ("seq", "kvh")),
    )
    out_specs = P("rep", ("seq", "kvh"))
    run = functools.partial(body, mesh.shape["seq"], mesh.shape["kvh"])
    return jax.shard_map(run, mesh=mesh, in_specs=in_specs, out_specs=out_specs, check_vma=False)
```

```python
import functools
import math

import jax
import jax.numpy as jnp
from jax import lax
from jax.experimental import pallas as pl
from jax.experimental.pallas import tpu as pltpu
from jax.sharding import PartitionSpec as P

BLOCK_POSITIONS = 32
MESH = pl.DeviceIdType.MESH


def partner(me, step, count):
    result = 0
    bit = 1
    while bit < count:
        own = lax.rem(lax.div(me, bit), 2)
        result = result + bit * (1 - own if (step // bit) % 2 else own)
        bit *= 2
    return result


def kernel(
    n_seq, n_kvh,
    lengths, queries, keys, values, weights, residual, out,
    l_buf, q_buf, q_rows, k_buf, v_buf, w_buf, r_buf,
    part_send, part_recv, direct_send, direct_recv, contrib,
    load_sem, ps_sem, pr_sem, ds_sem, dr_sem,
):
    seq = lax.axis_index("seq")
    kvh = lax.axis_index("kvh")
    rows, _, heads, size = queries.shape
    slots = keys.shape[2]
    share = out.shape[1]
    blocks = n_seq * n_kvh

    loads = {
        "keys": pltpu.make_async_copy(keys, k_buf, load_sem.at[0]),
        "queries": pltpu.make_async_copy(queries, q_buf, load_sem.at[1]),
        "lengths": pltpu.make_async_copy(lengths, l_buf, load_sem.at[2]),
        "values": pltpu.make_async_copy(values, v_buf, load_sem.at[3]),
        "weights": pltpu.make_async_copy(weights.at[0, 0], w_buf, load_sem.at[4]),
        "residual": pltpu.make_async_copy(residual, r_buf, load_sem.at[5]),
    }
    for name in ("keys", "queries", "lengths", "values"):
        loads[name].start()

    seq_peers = [partner(seq, i, n_seq) for i in range(n_seq)]
    kvh_peers = [partner(kvh, j, n_kvh) for j in range(n_kvh)]
    barrier = pltpu.get_barrier_semaphore()
    greeted = 0
    for i in range(n_seq):
        for j in range(n_kvh):
            if i or j:
                target = {"seq": seq_peers[i], "kvh": kvh_peers[j]}
                pl.semaphore_signal(barrier, inc=1, device_id=target, device_id_type=MESH)
                greeted += 1

    row = lax.broadcasted_iota(jnp.int32, (rows, slots), 0)
    slot = lax.broadcasted_iota(jnp.int32, (rows, slots), 1)
    length = jnp.zeros((rows, slots), jnp.int32)
    loads["lengths"].wait()
    for b in range(rows):
        length = jnp.where(row == b, l_buf[b], length)
    position = (slot // BLOCK_POSITIONS * n_seq + seq) * BLOCK_POSITIONS + slot % BLOCK_POSITIONS
    live = position < length
    out_row = lax.broadcasted_iota(jnp.int32, (rows, size), 0)

    loads["queries"].wait()
    for b in range(rows):
        q_rows[pl.ds(b * heads, heads), :] = q_buf[b, 0].astype(jnp.float32)
    q = jnp.concatenate(
        [q_rows[pl.ds(g, rows, stride=heads), :] for g in range(heads)], axis=0
    ).astype(jnp.bfloat16)

    loads["keys"].wait()
    loads["weights"].start()
    scores = jnp.zeros((heads, rows, slots), jnp.float32)
    for b in range(rows):
        full = lax.dot_general(
            q, k_buf[b, 0], (((1,), (1,)), ((), ())), preferred_element_type=jnp.float32
        ).reshape(heads, rows, slots)
        scores = jnp.where((row == b)[None], full, scores)
    scores = jnp.where(live[None], scores * (1.0 / math.sqrt(size)), -1e30)
    top = jnp.max(scores, axis=2, keepdims=True)
    probs = jnp.exp(scores - top)
    total = jnp.sum(probs, axis=2, keepdims=True)
    probs = probs.reshape(heads * rows, slots).astype(jnp.bfloat16)
    loads["values"].wait()
    summed = jnp.zeros((heads, rows, size), jnp.float32)
    for b in range(rows):
        full = jnp.dot(probs, v_buf[b, 0], preferred_element_type=jnp.float32)
        summed = jnp.where((out_row == b)[None], full.reshape(heads, rows, size), summed)
    part_send[:, :rows, :] = summed / total
    part_send[:, rows:, :] = jnp.broadcast_to(top + jnp.log(total), (heads, rows, size))

    pl.semaphore_wait(barrier, greeted)
    order = list(range(n_seq - 1, 0, -1))
    for i in order:
        pltpu.make_async_remote_copy(
            src_ref=part_send.at[seq_peers[i]],
            dst_ref=part_recv.at[i - 1],
            send_sem=ps_sem,
            recv_sem=pr_sem,
            device_id={"seq": seq_peers[i]},
            device_id_type=MESH,
        ).start()

    loads["residual"].start()
    loads["weights"].wait()
    pltpu.make_async_copy(part_recv, part_recv, pr_sem).wait()
    parts = [part_send[seq]] + [part_recv[i] for i in range(n_seq - 1)]
    highest = functools.reduce(jnp.maximum, [part[rows:] for part in parts])
    factors = [jnp.exp(part[rows:] - highest) for part in parts]
    joined = sum(factor * part[:rows] for factor, part in zip(factors, parts))
    attended = (joined / sum(factors)).astype(jnp.bfloat16)

    aligned = share % 128 == 0
    if not aligned:
        for first in range(0, blocks * share, 1024):
            tile = jnp.dot(
                attended, w_buf[:, first:first + 1024], preferred_element_type=jnp.float32
            )
            for block in range(1024 // share):
                contrib[first // share + block] = tile[:, block * share:(block + 1) * share]

    def contribution(block):
        if not aligned:
            return contrib[block]
        columns = pl.ds(pl.multiple_of(block * share, 128), share)
        return jnp.dot(attended, w_buf[:, columns], preferred_element_type=jnp.float32)

    pairs = [(i, j) for j in range(n_kvh) for i in order] + [(0, j) for j in range(1, n_kvh)]
    done = 0
    while done < len(pairs):
        group = pairs[done:2 * done + 1]
        done += len(group)
        for i, j in group:
            direct_send[i * n_kvh + j - 1] = contribution(seq_peers[i] * n_kvh + kvh_peers[j])
        for i, j in group:
            slot = i * n_kvh + j - 1
            pltpu.make_async_remote_copy(
                src_ref=direct_send.at[slot],
                dst_ref=direct_recv.at[slot],
                send_sem=ds_sem,
                recv_sem=dr_sem,
                device_id={"seq": seq_peers[i], "kvh": kvh_peers[j]},
                device_id_type=MESH,
            ).start()
    loads["residual"].wait()
    result = r_buf[...] + contribution(seq * n_kvh + kvh)
    pltpu.make_async_copy(part_recv, part_recv, ps_sem).wait()
    pltpu.make_async_copy(direct_recv, direct_recv, dr_sem).wait()
    for slot in range(blocks - 1):
        result = result + direct_recv[slot]
    out[...] = result
    pltpu.make_async_copy(direct_send, direct_send, ds_sem).wait()


def body(n_seq, n_kvh, queries, keys, values, lengths, weights, residual):
    rows, _, heads, size = queries.shape
    slots = keys.shape[2]
    features = weights.shape[3]
    share = residual.shape[1]
    f32, bf16 = jnp.float32, jnp.bfloat16
    dma = pltpu.SemaphoreType.DMA
    in_hbm = pl.BlockSpec(memory_space=pltpu.HBM)
    return pl.pallas_call(
        functools.partial(kernel, n_seq, n_kvh),
        out_shape=jax.ShapeDtypeStruct((rows, share), f32),
        in_specs=[in_hbm] * 6,
        out_specs=pl.BlockSpec(memory_space=pltpu.VMEM),
        scratch_shapes=[
            pltpu.SMEM((rows,), jnp.int32),
            pltpu.VMEM((rows, 1, heads, size), bf16),
            pltpu.VMEM((rows * heads, size), f32),
            pltpu.VMEM((rows, 1, slots, size), bf16),
            pltpu.VMEM((rows, 1, slots, size), bf16),
            pltpu.VMEM((size, features), bf16),
            pltpu.VMEM((rows, share), f32),
            pltpu.VMEM((heads, 2 * rows, size), f32),
            pltpu.VMEM((n_seq - 1, 2 * rows, size), f32),
            pltpu.VMEM((n_seq * n_kvh - 1, rows, share), f32),
            pltpu.VMEM((n_seq * n_kvh - 1, rows, share), f32),
            pltpu.VMEM((n_seq * n_kvh if share % 128 else 1, rows, share), f32),
            dma((6,)),
            dma,
            dma,
            dma,
            dma,
        ],
        compiler_params=pltpu.CompilerParams(
            collective_id=0, has_side_effects=True, vmem_limit_bytes=40 * 1024 * 1024
        ),
        cost_estimate=pl.CostEstimate(
            flops=2 * rows * size * features, bytes_accessed=2 * size * features, transcendentals=0
        ),
    )(*[
        pltpu.with_memory_space_constraint(array, pltpu.HBM)
        for array in (lengths, queries, keys, values, weights, residual)
    ])


def solution(mesh):
    in_specs = (
        P("rep", "kvh", None, None),
        P("rep", "kvh", "seq", None),
        P("rep", "kvh", "seq", None),
        P("rep"),
        P("kvh", "seq", None, None),
        P("rep", ("seq", "kvh")),
    )
    out_specs = P("rep", ("seq", "kvh"))
    run = functools.partial(body, mesh.shape["seq"], mesh.shape["kvh"])
    return jax.shard_map(run, mesh=mesh, in_specs=in_specs, out_specs=out_specs, check_vma=False)
```
